256 devices in a mesh: dp: 32 (over z, y), mp: 8 (over x, core).
Axes of the slice: x: 4, y: 4, z: 8, core: 2. Of those that a mesh axis runs over, the one named last changes fastest.
Arguments:
- queries: bfloat16 [12288, 4096], P('dp', 'mp'), may hold values from -16 to 16
- states: bfloat16 [256, 128, 896], P('dp', 'mp'), may hold values from -6 to 6
- key_weight: bfloat16 [896, 4096], P(None, 'mp'), may hold values from -0.1875 to 0.1875
- value_weight: bfloat16 [896, 4096], P(None, 'mp'), may hold values from -0.1875 to 0.1875
- nbr_shard: int32 [192, 2], P('dp'), may hold values from 0 to 31, all different within a row; in each aligned block of 6 rows (0 to 5, 6 to 11, ...) at most 2 rows name the same one
- nbr_row: int32 [192, 2], P('dp'), may hold values from 0 to 7
- out_grad: bfloat16 [12288, 4096], P('dp', 'mp'), may hold values from -6 to 6
Outputs:
- attended: bfloat16 [12288, 4096], P('dp', 'mp')
- query_grad: bfloat16 [12288, 4096], P('dp', 'mp')
- state_grad: float32 [256, 128, 896], P('dp', 'mp')
- key_weight_grad: float32 [896, 4096], P(None, 'mp')
- value_weight_grad: float32 [896, 4096], P(None, 'mp')
The draws below stay inside these ranges and needn't reach their ends.
Inputs may be any that keep to these rules, and one draw needn't show every extreme that they name: `nbr_shard`: the 2 neighbours of a span lie on different shards; among the 6 spans of one device at most 2 neighbours lie on one shard, and some shard takes exactly 2 of them.
All inputs are finite; a program needn't handle non-finite values.
Results may differ from the reference program's by a relative error of at most 0.02.
Values may be sent and summed in bfloat16 or wider, within the bound.
A program may use at most 128 MiB of HBM per device.

```python
import math
import jax
import jax.numpy as jnp
import numpy as np
from jax import lax

D = 4096
H = 32
E = 896
HD = 128
SPAN = 64
NLEN = 128
K = 2
C_DEV = 6
NB_DEV = 8
CAP = 2
SHARDS = 32
SPANS = 192
TOKENS = 12288
NBRS = 256
N_MP = 8


def draw_queries(key, part):
    key = jax.random.fold_in(key, 7)
    first = jax.random.fold_in(key, 0)
    values = jax.random.truncated_normal(first, -4.0, 4.0, (TOKENS, D), jnp.float32)
    return values.astype(jnp.bfloat16)


def with_ends(result, key, least, top_value):
    shape = result.shape
    place = [jax.random.randint(jax.random.fold_in(key, axis), (), 0, shape[axis]) for axis in range(len(shape))]
    result = result.at[tuple(place)].set(least)
    longest = shape.index(max(shape))
    place[longest] = (place[longest] + 1) % shape[longest]
    return result.at[tuple(place)].set(top_value)


def block_scale(key, dims, cuts, smallest, top_value):
    def one(position, blocks):
        steps = jax.random.uniform(jax.random.fold_in(jax.random.fold_in(key, 6), position), (blocks,), jnp.float32, smallest / len(cuts), top_value / len(cuts))
        return jnp.repeat(jnp.exp(steps), dims[position] // blocks).reshape((-1,) + (1,) * (len(dims) - position - 1))

    gain = one(*cuts[0])
    for cut in cuts[1:]:
        gain = gain * one(*cut)
    return gain


def routed_block(rng, own, number, rows, amount, top, most, lean):
    ranking = jax.random.permutation(rng, amount)
    heavy_load, usual = shares(amount, rows * top, most, lean, True), shares(amount, rows * top, most, lean, False)
    places = jnp.arange(amount)

    def named(lengths, turn):
        used = int((lengths > 0).sum())
        fixed = max(1, used // 4)
        shifted = fixed + (places - fixed + turn * (used - fixed)) % max(1, amount - fixed)
        return jnp.zeros((amount,), jnp.int32).at[ranking[jnp.where(places < fixed, places, shifted)]].set(jnp.asarray(lengths, jnp.int32))

    lengths = jnp.where(number % 4 == 0, named(heavy_load, number // 4), named(usual, number - number // 4 - 1))
    mixed = jax.random.permutation(jax.random.fold_in(own, 3), amount)
    donor, sink = mixed[0:amount // 2 * 2:2], mixed[1:amount // 2 * 2:2]
    margin = jnp.minimum(lengths[donor] - 1, most - lengths[sink]) // 2
    margin = jnp.where((donor == ranking[0]) | (sink == ranking[0]) | (lengths[sink] == 0), 0, jnp.maximum(margin, 0))
    shifted = jax.random.randint(jax.random.fold_in(own, 4), (amount // 2,), 0, 1 << 20) % (margin + 1)
    lengths = lengths.at[donor].add(-shifted).at[sink].add(shifted)
    items = jnp.searchsorted(jnp.cumsum(lengths), jnp.arange(rows * top), side="right").astype(jnp.int32)
    listing = items.reshape(top, rows).T
    listing = listing[jax.random.permutation(jax.random.fold_in(own, 1), rows)]
    turn = jax.random.randint(jax.random.fold_in(own, 2), (rows, 1), 0, top)
    return jnp.take_along_axis(listing, (jnp.arange(top)[None, :] + turn) % top, axis=1)


def shares(count, total, bound, lean, full):
    loads = [(1 << 20) // math.isqrt(standing ** lean) + 1 for standing in range(1, count + 1)]
    largest = bound if full else min(bound, max(-(-total // count), total * loads[0] // sum(loads)))
    least = 1 if total - largest >= count - 1 else 0
    given, rest = [largest] + [least] * (count - 1), total - largest - least * (count - 1)
    while rest > 0:
        free = [i for i in range(1, count) if given[i] < largest] or [i for i in range(1, count) if given[i] < bound]
        whole, left = sum([loads[i] for i in free]), rest
        for i in free:
            extra = min(bound - given[i], max(1, left * loads[i] // whole), rest)
            given[i] = given[i] + extra
            rest = rest - extra
    return np.array(given)


def gaussian(rng, dims, scale, reach, cuts=(), held_as=jnp.bfloat16):
    array = jax.random.normal(rng, dims, jnp.float32) * scale
    if len(cuts) > 0:
        array = block_scale(rng, dims, cuts, -0.22, 0.18) * array
    return jnp.clip(array, min=-reach, max=reach).astype(held_as)


def setup_inputs(seed: int = 0) -> dict:
    streams_of = jax.random.split(jax.random.key(seed), 8)
    queries = draw_queries(jax.random.fold_in(streams_of[7], 71), 0)
    states = gaussian(streams_of[1], (NBRS, NLEN, E), 1.0, 6.0, ((0, 32), (1, 8)))
    key_weight = gaussian(streams_of[2], (E, D), E ** -0.5, 0.1875, ((1, 8),))
    value_weight = gaussian(streams_of[3], (E, D), E ** -0.5, 0.1875, ((1, 8),))
    nbr_shard_keys = jax.random.split(jax.random.fold_in(streams_of[4], 1), SPANS // C_DEV)
    nbr_shard_turns = jax.random.permutation(jax.random.fold_in(streams_of[4], 3), SPANS // C_DEV)
    nbr_shard = jax.vmap(lambda own, number: routed_block(jax.random.fold_in(streams_of[4], 2), own, number, C_DEV, SHARDS, K, CAP, 2))(nbr_shard_keys, nbr_shard_turns).reshape((SPANS, K))
    nbr_row = with_ends(jax.random.randint(streams_of[5], (SPANS, K), 0, NB_DEV), jax.random.fold_in(streams_of[5], 1), 0, NB_DEV - 1).astype(jnp.int32)
    out_grad = gaussian(streams_of[6], (TOKENS, D), 1.0, 6.0, ((0, 32), (1, 8)))
    return dict(queries=queries, states=states, key_weight=key_weight, value_weight=value_weight, nbr_shard=nbr_shard, nbr_row=nbr_row, out_grad=out_grad)


def reference(queries, states, key_weight, value_weight, nbr_shard, nbr_row, out_grad):
    score_scale = 1.0 / (HD ** 0.5)
    group_cols = D // N_MP
    neighbour_ids = (nbr_shard * NB_DEV + nbr_row).astype(jnp.int32)
    query_heads = queries.reshape(SPANS, SPAN, H, HD)
    grad_heads = out_grad.reshape(SPANS, SPAN, H, HD)
    key_groups = key_weight.astype(jnp.float32).reshape(E, N_MP, group_cols)
    value_groups = value_weight.astype(jnp.float32).reshape(E, N_MP, group_cols)

    def one_span(carry, inputs):
        key_wgrad, value_wgrad, state_total = carry
        span_ids, query_span, grad_span = inputs
        rows_flat = states[span_ids].reshape(K * NLEN, E)
        key_rows = jnp.dot(rows_flat, key_weight, preferred_element_type=jnp.float32).astype(jnp.bfloat16)
        value_rows = jnp.dot(rows_flat, value_weight, preferred_element_type=jnp.float32).astype(jnp.bfloat16)
        key_heads = key_rows.reshape(K * NLEN, H, HD).astype(jnp.float32)
        value_heads = value_rows.reshape(K * NLEN, H, HD).astype(jnp.float32)
        query_f = query_span.astype(jnp.float32)
        grad_f = grad_span.astype(jnp.float32)
        scores = jnp.einsum('qhd,khd->hqk', query_f, key_heads) * score_scale
        probs = jax.nn.softmax(scores, axis=-1)
        probs_low = probs.astype(jnp.bfloat16)
        attended = jnp.einsum('hqk,khd->qhd', probs_low.astype(jnp.float32), value_heads).astype(jnp.bfloat16)
        prob_grad = jnp.einsum('qhd,khd->hqk', grad_f, value_heads)
        row_dot = jnp.sum(probs * prob_grad, axis=-1, keepdims=True)
        score_grad = (score_scale * probs * (prob_grad - row_dot)).astype(jnp.bfloat16)
        score_f = score_grad.astype(jnp.float32)
        query_grad = jnp.einsum('hqk,khd->qhd', score_f, key_heads).astype(jnp.bfloat16)
        key_grad = jnp.einsum('hqk,qhd->khd', score_f, query_f).astype(jnp.bfloat16).reshape(K * NLEN, D)
        value_grad = jnp.einsum('hqk,qhd->khd', probs_low.astype(jnp.float32), grad_f).astype(jnp.bfloat16).reshape(K * NLEN, D)
        key_wgrad = key_wgrad + jnp.dot(rows_flat.T, key_grad, preferred_element_type=jnp.float32)
        value_wgrad = value_wgrad + jnp.dot(rows_flat.T, value_grad, preferred_element_type=jnp.float32)
        key_split = key_grad.astype(jnp.float32).reshape(K * NLEN, N_MP, group_cols)
        value_split = value_grad.astype(jnp.float32).reshape(K * NLEN, N_MP, group_cols)
        head_part = jnp.einsum('tgd,egd->gte', key_split, key_groups) + jnp.einsum('tgd,egd->gte', value_split, value_groups)
        head_low = lax.optimization_barrier(head_part.astype(jnp.bfloat16))
        pair_grad = jnp.sum(head_low.astype(jnp.float32), axis=0).astype(jnp.bfloat16)
        state_total = state_total.at[span_ids].add(pair_grad.reshape(K, NLEN, E).astype(jnp.float32))
        return (key_wgrad, value_wgrad, state_total), (attended, query_grad)

    start = (jnp.zeros((E, D), jnp.float32), jnp.zeros((E, D), jnp.float32), jnp.zeros((NBRS, NLEN, E), jnp.float32))
    finals, outputs = lax.scan(one_span, start, (neighbour_ids, query_heads, grad_heads))
    key_wgrad, value_wgrad, state_total = finals
    attended = outputs[0].reshape(TOKENS, D)
    query_grad = outputs[1].reshape(TOKENS, D)
    return (attended, query_grad, state_total, key_wgrad, value_wgrad)
```

```python
import functools

import jax
import jax.numpy as jnp
from jax import lax
from jax.experimental import pallas as pl
from jax.experimental.pallas import tpu as pltpu
from jax.sharding import PartitionSpec as P

D = 4096
H = 32
HD = 128
NZ, NY, NX = 8, 4, 4
GROUPS = 8
SLOTS = 12
HALF = SLOTS // 2
ROWS = 8
TOK = 16
E = 896
CHUNKS = ((0, 512), (512, 384))
VMEM_LIMIT = 56 * 1024 * 1024
BF16 = jnp.bfloat16
F32 = jnp.float32


class Place:
    def __init__(self):
        dp, mp = lax.axis_index("dp"), lax.axis_index("mp")
        self.dp, self.mp = dp, mp
        self.z, self.y = dp // NY, lax.rem(dp, NY)
        self.x, self.core = mp // 2, lax.rem(mp, 2)

    def zi(self, k):
        return lax.rem(self.z + (k + NZ), NZ)

    def yi(self, k):
        return lax.rem(self.y + (k + NY), NY)

    def xi(self, k):
        return lax.rem(self.x + (k + NX), NX)

    def at_z(self, k):
        return (self.zi(k) * NY + self.y, self.mp)

    def at_y(self, k):
        return (self.z * NY + self.yi(k), self.mp)

    def at_x(self, k):
        return (self.dp, self.xi(k) * 2 + self.core)

    def sibling(self):
        return (self.dp, self.x * 2 + (1 - self.core))

    def partners(self):
        return [
            self.at_z(1), self.at_z(-1), self.at_y(1), self.at_y(-1), self.at_y(2),
            self.at_x(1), self.at_x(-1), self.sibling(),
        ]


class Net:
    def __init__(self, send_sems, recv_sems, local_sems):
        self.send_sems, self.recv_sems, self.local_sems = send_sems, recv_sems, local_sems
        self.sent = []
        self.locals = 0

    def send(self, src, dst, device):
        number = len(self.sent)
        copy = pltpu.make_async_remote_copy(
            src_ref=src,
            dst_ref=dst,
            send_sem=self.send_sems.at[number],
            recv_sem=self.recv_sems.at[number],
            device_id=device,
            device_id_type=pl.DeviceIdType.MESH,
        )
        copy.start()
        self.sent.append(copy)
        return copy

    def local(self, src, dst):
        copy = pltpu.make_async_copy(src, dst, self.local_sems.at[self.locals])
        copy.start()
        self.locals += 1
        return copy

    def finish(self):
        for copy in self.sent:
            copy.wait_send()


def greet(place):
    barrier = pltpu.get_barrier_semaphore()
    partners = place.partners()
    for device in partners:
        pl.semaphore_signal(barrier, inc=1, device_id=device, device_id_type=pl.DeviceIdType.MESH)
    pl.semaphore_wait(barrier, len(partners))


def run_chains(chains):
    live = list(chains)
    turn = 0
    while live:
        rest = []
        for first, chain in live:
            if turn >= first:
                try:
                    next(chain)
                except StopIteration:
                    continue
            rest.append((first, chain))
        live = rest
        turn += 1


def part(ref, bounds):
    first, count = bounds
    return ref.at[pl.ds(first, count)]


def ring_gather(net, n, right, left, slot, halves, landed=None):
    half_r, half_l = halves
    whole = (half_r[0], half_r[1] + half_l[1])
    far = n // 2
    for step in range(1, far + 1):
        piece_r = half_r if step == far else whole
        piece_l = half_l if step == far else whole
        block_r, block_l = part(slot(1 - step), piece_r), part(slot(step - 1), piece_l)
        to_right = net.send(block_r, block_r, right)
        to_left = net.send(block_l, block_l, left)
        yield
        to_right.wait_recv()
        if landed is not None:
            landed(part(slot(-step), piece_r))
        to_left.wait_recv()
        if landed is not None:
            landed(part(slot(step), piece_l))


def add_into(target, *others):
    total = target[...].astype(F32)
    for other in others:
        total = total + other[...].astype(F32)
    target[...] = total.astype(target.dtype)


def ring_scatter(net, n, right, left, total, prepare, from_left, from_right, halves):
    half_r, half_l = halves
    whole = (half_r[0], half_r[1] + half_l[1])
    far = n // 2
    prepare(far)
    to_right = [net.send(part(total(far), half_r), part(from_left(0), half_r), right)]
    to_left = [net.send(part(total(far), half_l), part(from_right(0), half_l), left)]
    for step in range(1, far):
        k = far - step
        prepare(k)
        prepare(-k)
        early_r, early_l = [], []
        if step == 1:
            early_r.append(net.send(part(total(k), half_l), part(from_left(step), half_l), right))
            early_l.append(net.send(part(total(-k), half_r), part(from_right(step), half_r), left))
        piece_r = half_r if step == 1 else whole
        piece_l = half_l if step == 1 else whole
        yield
        for copy in to_right:
            copy.wait_recv()
        add_into(part(total(k), piece_r), part(from_left(step - 1), piece_r))
        to_right = early_r + [net.send(part(total(k), piece_r), part(from_left(step), piece_r), right)]
        for copy in to_left:
            copy.wait_recv()
        add_into(part(total(-k), piece_l), part(from_right(step - 1), piece_l))
        to_left = early_l + [net.send(part(total(-k), piece_l), part(from_right(step), piece_l), left)]
    prepare(0)
    yield
    for copy in to_right + to_left:
        copy.wait_recv()
    add_into(total(0), from_left(far - 1), from_right(far - 1))


SLOT_HALVES = ((0, HALF), (HALF, HALF))
ROW_HALVES = ((0, ROWS // 2), (ROWS // 2, ROWS // 2))


FWD_COPIES = 96
FWD_LOCALS = 16


def fwd_kernel(meta_in, states, *refs):
    count = len(CHUNKS)
    outs, refs = refs[:count], refs[count:]
    meta_out, refs = refs[0], refs[1:]
    per_chunk = [refs[6 * i:6 * i + 6] for i in range(count)]
    meta_v, meta_s, send_sems, recv_sems, local_sems = refs[6 * count:]
    place = Place()
    net = Net(send_sems, recv_sems, local_sems)
    own_meta = net.local(meta_in, meta_v.at[place.y])
    loads = []
    for (first, width), bufs in zip(CHUNKS, per_chunk):
        loads.append(net.local(states.at[:, :, pl.ds(first, width)], bufs[0].at[place.z]))
    greet(place)

    def meta_chain():
        copies = [net.send(meta_in, meta_v.at[place.y], place.at_y(k)) for k in (1, -1, 2)]
        yield
        own_meta.wait()
        for copy in copies:
            copy.wait_recv()
        to_smem = net.local(meta_v, meta_s)
        to_out = net.local(meta_v, meta_out)
        to_smem.wait()
        to_out.wait()

    def chunk_chain(i):
        zbuf, send1, recv1, send2, recv2, rows = per_chunk[i]
        first, width = CHUNKS[i]
        loads[i].wait()
        yield from ring_gather(
            net, NZ, place.at_z(1), place.at_z(-1), lambda k: zbuf.at[place.zi(k)], ROW_HALVES
        )
        yield
        y, right, left = place.y, place.at_y(1), place.at_y(-1)

        def held(k, j):
            dest = place.yi(k)
            entry = meta_s[dest, 0, j]
            return zbuf[entry // ROWS, lax.rem(entry, ROWS)]

        def column(k, j):
            return meta_s[place.yi(k), 1, j]

        for j in range(HALF):
            send1[0, j] = held(2, j)
            send1[1, j] = held(2, j + HALF)
        one_r = net.send(send1.at[0], recv1.at[0], right)
        one_l = net.send(send1.at[1], recv1.at[1], left)
        for j in range(HALF):
            send2[0, j + HALF] = held(1, j + HALF)
            send2[1, j] = held(-1, j)
        two_r = net.send(send2.at[0, pl.ds(HALF, HALF)], recv2.at[0, pl.ds(HALF, HALF)], right)
        two_l = net.send(send2.at[1, pl.ds(0, HALF)], recv2.at[1, pl.ds(0, HALF)], left)
        yield
        one_r.wait_recv()
        for j in range(HALF):
            send2[0, j] = lax.select(column(1, j) == y, held(1, j), recv1[0, j])
        three_r = net.send(send2.at[0, pl.ds(0, HALF)], recv2.at[0, pl.ds(0, HALF)], right)
        one_l.wait_recv()
        for j in range(HALF):
            send2[1, j + HALF] = lax.select(column(-1, j + HALF) == y, held(-1, j + HALF), recv1[1, j])
        three_l = net.send(send2.at[1, pl.ds(HALF, HALF)], recv2.at[1, pl.ds(HALF, HALF)], left)
        yield
        for copy in (two_r, two_l, three_r, three_l):
            copy.wait_recv()
        mp = place.mp
        for j in range(SLOTS):
            own_column = column(0, j)
            by_left = own_column == place.yi(-1)
            if j < HALF:
                by_left = jnp.logical_or(by_left, own_column == place.yi(2))
            other = lax.select(by_left, recv2[0, j], recv2[1, j])
            rows[j, mp] = lax.select(own_column == y, held(0, j), other)
        across = []

        def landed(block):
            across.append(net.send(block, block, place.sibling()))

        def slot(k):
            return rows.at[:, place.xi(k) * 2 + place.core]

        landed(slot(0))
        yield from ring_gather(net, NX, place.at_x(1), place.at_x(-1), slot, SLOT_HALVES, landed)
        yield
        for copy in across:
            copy.wait_recv()
        done = net.local(rows, outs[i])
        yield
        done.wait()

    run_chains([(0, meta_chain())] + [(2 * i, chunk_chain(i)) for i in range(count)])
    net.finish()


def forward(meta, states):
    scratch = []
    for _, width in CHUNKS:
        scratch += [
            pltpu.VMEM((NZ, ROWS, TOK, width), BF16),
            pltpu.VMEM((2, HALF, TOK, width), BF16),
            pltpu.VMEM((2, HALF, TOK, width), BF16),
            pltpu.VMEM((2, SLOTS, TOK, width), BF16),
            pltpu.VMEM((2, SLOTS, TOK, width), BF16),
            pltpu.VMEM((SLOTS, GROUPS, TOK, width), BF16),
        ]
    scratch += [
        pltpu.VMEM((NY, 8, 128), jnp.int32),
        pltpu.SMEM((NY, 8, 128), jnp.int32),
        pltpu.SemaphoreType.DMA((FWD_COPIES,)),
        pltpu.SemaphoreType.DMA((FWD_COPIES,)),
        pltpu.SemaphoreType.DMA((FWD_LOCALS,)),
    ]
    return pl.pallas_call(
        fwd_kernel,
        out_shape=[jax.ShapeDtypeStruct((SLOTS, GROUPS, TOK, w), BF16) for _, w in CHUNKS]
        + [jax.ShapeDtypeStruct((NY, 8, 128), jnp.int32)],
        in_specs=[pl.BlockSpec(memory_space=pltpu.VMEM), pl.BlockSpec(memory_space=pl.ANY)],
        out_specs=[pl.BlockSpec(memory_space=pl.ANY)] * (len(CHUNKS) + 1),
        scratch_shapes=scratch,
        compiler_params=pltpu.CompilerParams(
            collective_id=0, has_side_effects=True, vmem_limit_bytes=VMEM_LIMIT
        ),
        name="gather_slabs",
    )(meta, states)


SPAN_LEN = 64
STEP_SPANS = 2
LOCAL = 512
HEADS = LOCAL // HD


def mm(a, b, dims):
    return lax.dot_general(a, b, (dims, ((), ())), preferred_element_type=F32)


def attend_kernel(q, g, kw, vw, *refs):
    count = len(CHUNKS)
    row_refs, refs = refs[:count], refs[count:]
    att, qg = refs[0], refs[1]
    state_outs, refs = refs[2:2 + count], refs[2 + count:]
    kgrad, vgrad, total = refs
    step = pl.program_id(0)
    tokens = STEP_SPANS * 2 * 128
    scale = 1.0 / HD**0.5
    rows = [ref[...].reshape(tokens, w) for ref, (_, w) in zip(row_refs, CHUNKS)]

    def project(weight):
        out = None
        for piece, (first, width) in zip(rows, CHUNKS):
            term = mm(piece, weight[pl.ds(first, width), :], ((1,), (0,)))
            out = term if out is None else out + term
        return out.astype(BF16)

    keys, values = project(kw), project(vw)
    key_parts, value_parts = [], []
    for c in range(STEP_SPANS):
        key_heads, value_heads = [], []
        for h in range(HEADS):
            cols = slice(h * HD, (h + 1) * HD)
            span = slice(c * SPAN_LEN, (c + 1) * SPAN_LEN)
            span_rows = slice(c * 256, (c + 1) * 256)
            qh, gh = q[span, cols], g[span, cols]
            kh, vh = keys[span_rows, cols], values[span_rows, cols]
            scores = mm(qh, kh, ((1,), (1,))) * scale
            top = jnp.max(scores, axis=-1, keepdims=True)
            grown = jnp.exp(scores - top)
            probs = grown / jnp.sum(grown, axis=-1, keepdims=True)
            low = probs.astype(BF16)
            att[span, cols] = mm(low, vh, ((1,), (0,))).astype(BF16)
            pgrad = mm(gh, vh, ((1,), (1,)))
            dot = jnp.sum(probs * pgrad, axis=-1, keepdims=True)
            sgrad = (scale * probs * (pgrad - dot)).astype(BF16)
            qg[span, cols] = mm(sgrad, kh, ((1,), (0,))).astype(BF16)
            key_heads.append(mm(sgrad, qh, ((0,), (0,))).astype(BF16))
            value_heads.append(mm(low, gh, ((0,), (0,))).astype(BF16))
        key_parts.append(jnp.concatenate(key_heads, axis=1))
        value_parts.append(jnp.concatenate(value_heads, axis=1))
    kg, vg = jnp.concatenate(key_parts, axis=0), jnp.concatenate(value_parts, axis=0)
    for ref, (first, width) in zip(state_outs, CHUNKS):
        piece = pl.ds(first, width)
        term = mm(kg, kw[piece, :], ((1,), (1,))) + mm(vg, vw[piece, :], ((1,), (1,)))
        ref[...] = term.astype(BF16).reshape(ref.shape)

    @pl.when(step == 0)
    def _():
        total[...] = jnp.zeros_like(total)

    for piece, (first, width) in zip(rows, CHUNKS):
        at = pl.ds(first, width)
        total[at, pl.ds(0, LOCAL)] += mm(piece, kg, ((0,), (0,)))
        total[at, pl.ds(LOCAL, LOCAL)] += mm(piece, vg, ((0,), (0,)))

    @pl.when(step == pl.num_programs(0) - 1)
    def _():
        for z in range(NZ):
            for h in range(HEADS):
                at = pl.ds(z * WROWS, WROWS)
                kgrad[z, h] = total[at, pl.ds(h * HD, HD)].astype(BF16)
                vgrad[z, h] = total[at, pl.ds(LOCAL + h * HD, HD)].astype(BF16)


WROWS = E // NZ


def attend(queries, out_grad, key_weight, value_weight, rows):
    steps = queries.shape[0] // (STEP_SPANS * SPAN_LEN)
    slots = STEP_SPANS * 2
    token_spec = pl.BlockSpec((STEP_SPANS * SPAN_LEN, LOCAL), lambda i: (i, 0))
    weight_spec = pl.BlockSpec((E, LOCAL), lambda i: (0, 0))
    row_specs = [pl.BlockSpec((slots, GROUPS, TOK, w), lambda i: (i, 0, 0, 0)) for _, w in CHUNKS]
    grad_spec = pl.BlockSpec((NZ, HEADS, WROWS, HD), lambda i: (0, 0, 0, 0))
    grad_shape = jax.ShapeDtypeStruct((NZ, HEADS, WROWS, HD), BF16)
    return pl.pallas_call(
        attend_kernel,
        grid=(steps,),
        out_shape=[jax.ShapeDtypeStruct(queries.shape, BF16)] * 2
        + [jax.ShapeDtypeStruct((SLOTS, GROUPS, TOK, w), BF16) for _, w in CHUNKS]
        + [grad_shape] * 2,
        in_specs=[token_spec, token_spec, weight_spec, weight_spec] + row_specs,
        out_specs=[token_spec, token_spec] + row_specs + [grad_spec] * 2,
        scratch_shapes=[pltpu.VMEM((E, 2 * LOCAL), F32)],
        compiler_params=pltpu.CompilerParams(vmem_limit_bytes=VMEM_LIMIT),
        name="attend",
    )(queries, out_grad, key_weight, value_weight, *rows)


BWD_COPIES = 160
BWD_LOCALS = 24
HEAD_HALVES = ((0, HEADS // 2), (HEADS // 2, HEADS // 2))
ZBLOCK_HALVES = ((0, NZ // 2), (NZ // 2, NZ // 2))
WROW_HALVES = ((0, 64), (64, WROWS - 64))


def bwd_kernel(meta, *refs):
    count = len(CHUNKS)
    terms, refs = refs[:count], refs[count:]
    kgrad, vgrad, state_out, kout, vout = refs[:5]
    refs = refs[5:]
    per_chunk = [refs[8 * i:8 * i + 8] for i in range(count)]
    refs = refs[8 * count:]
    (kw, kfl, kfr, ky, kmine, kres, vw, vyl, vyr, vzl, vzr, vres, send_sems, recv_sems, local_sems) = refs
    place = Place()
    net = Net(send_sems, recv_sems, local_sems)
    order = (2, 1, -1, 0)
    loads = []
    for i in range(count):
        mine = per_chunk[i][0]
        loads.append(
            [net.local(terms[i].at[:, place.xi(k) * 2 + place.core], mine.at[n]) for n, k in enumerate(order)]
        )
    load_k, load_v = net.local(kgrad, kw), net.local(vgrad, vw)
    greet(place)

    def nothing(k):
        pass

    def state_chain(i):
        mine, theirs, xl, xr, ybuf, part_buf, zl, zr = per_chunk[i]
        first, width = CHUNKS[i]
        crossing = [
            net.send(terms[i].at[:, place.xi(k) * 2 + (1 - place.core)], theirs.at[n], place.sibling())
            for n, k in enumerate(order)
        ]
        yield

        def prepare_x(k):
            n = order.index(k)
            loads[i][n].wait()
            crossing[n].wait_recv()
            add_into(mine.at[n], theirs.at[n])

        yield from ring_scatter(
            net, NX, place.at_x(1), place.at_x(-1), lambda k: mine.at[order.index(k)], prepare_x,
            lambda s: xl.at[s], lambda s: xr.at[s], SLOT_HALVES,
        )
        ybuf[place.y] = mine[3]
        yield from ring_gather(
            net, NY, place.at_y(1), place.at_y(-1), lambda k: ybuf.at[place.yi(k)], SLOT_HALVES
        )

        def prepare_z(k):
            shard = place.zi(k) * NY + place.y
            where = (k + NZ) % NZ
            named = [
                (d, meta[d, 2, shard * 2 + r], meta[d, 3, shard * 2 + r]) for d in range(NY) for r in range(2)
            ]
            for row in range(ROWS):
                total = None
                for d, slot, slot_row in named:
                    weight = jnp.where(slot_row == row, 1.0, 0.0).astype(F32)
                    term = ybuf[d, slot].astype(F32) * weight
                    total = term if total is None else total + term
                part_buf[where, row] = total.astype(BF16)

        yield from ring_scatter(
            net, NZ, place.at_z(1), place.at_z(-1), lambda k: part_buf.at[(k + NZ) % NZ], prepare_z,
            lambda s: zl.at[s], lambda s: zr.at[s], ROW_HALVES,
        )
        state_out[:, :, pl.ds(first, width)] = part_buf[0].astype(F32)

    def key_chain():
        load_k.wait()
        yield from ring_scatter(
            net, NZ, place.at_z(1), place.at_z(-1), lambda k: kw.at[place.zi(k)], nothing,
            lambda s: kfl.at[s], lambda s: kfr.at[s], HEAD_HALVES,
        )
        own = kw.at[place.z]
        copies = [net.send(own.at[place.yi(k)], ky.at[n], place.at_y(k)) for n, k in enumerate((1, -1, 2))]
        yield
        for copy in copies:
            copy.wait_recv()
        kmine[...] = own[place.y]
        add_into(kmine, ky.at[0], ky.at[1], ky.at[2])
        spot = kres.at[place.z, place.y]
        copies = [net.send(kmine, spot, place.at_y(k)) for k in (1, -1, 2)]
        kres[place.z, place.y] = kmine[...]
        yield
        for copy in copies:
            copy.wait_recv()
        yield from ring_gather(
            net, NZ, place.at_z(1), place.at_z(-1), lambda k: kres.at[place.zi(k)], HEAD_HALVES
        )
        done = net.local(kres, kout)
        yield
        done.wait()

    def value_chain():
        load_v.wait()
        yield from ring_scatter(
            net, NY, place.at_y(1), place.at_y(-1), lambda k: vw.at[:, place.yi(k)], nothing,
            lambda s: vyl.at[s], lambda s: vyr.at[s], ZBLOCK_HALVES,
        )
        yield from ring_scatter(
            net, NZ, place.at_z(1), place.at_z(-1), lambda k: vw.at[place.zi(k), place.y], nothing,
            lambda s: vzl.at[s], lambda s: vzr.at[s], WROW_HALVES,
        )
        vres[place.z, place.y] = vw[place.z, place.y]
        yield from ring_gather(
            net, NZ, place.at_z(1), place.at_z(-1), lambda k: vres.at[place.zi(k), place.y], WROW_HALVES
        )
        yield from ring_gather(
            net, NY, place.at_y(1), place.at_y(-1), lambda k: vres.at[:, place.yi(k)], ZBLOCK_HALVES
        )
        done = net.local(vres, vout)
        yield
        done.wait()

    run_chains(
        [(2 * i, state_chain(i)) for i in range(count)] + [(0, key_chain()), (0, value_chain())]
    )
    net.finish()


def backward(meta, terms, kgrad, vgrad):
    scratch = []
    for _, width in CHUNKS:
        scratch += [
            pltpu.VMEM((NX, SLOTS, TOK, width), BF16),
            pltpu.VMEM((NX, SLOTS, TOK, width), BF16),
            pltpu.VMEM((2, SLOTS, TOK, width), BF16),
            pltpu.VMEM((2, SLOTS, TOK, width), BF16),
            pltpu.VMEM((NY, SLOTS, TOK, width), BF16),
            pltpu.VMEM((NZ, ROWS, TOK, width), BF16),
            pltpu.VMEM((NZ // 2, ROWS, TOK, width), BF16),
            pltpu.VMEM((NZ // 2, ROWS, TOK, width), BF16),
        ]
    scratch += [
        pltpu.VMEM((NZ, HEADS, WROWS, HD), BF16),
        pltpu.VMEM((NZ // 2, HEADS, WROWS, HD), BF16),
        pltpu.VMEM((NZ // 2, HEADS, WROWS, HD), BF16),
        pltpu.VMEM((3, WROWS, HD), BF16),
        pltpu.VMEM((WROWS, HD), BF16),
        pltpu.VMEM((NZ, HEADS, WROWS, HD), BF16),
        pltpu.VMEM((NZ, HEADS, WROWS, HD), BF16),
        pltpu.VMEM((NY // 2, NZ, WROWS, HD), BF16),
        pltpu.VMEM((NY // 2, NZ, WROWS, HD), BF16),
        pltpu.VMEM((NZ // 2, WROWS, HD), BF16),
        pltpu.VMEM((NZ // 2, WROWS, HD), BF16),
        pltpu.VMEM((NZ, HEADS, WROWS, HD), BF16),
        pltpu.SemaphoreType.DMA((BWD_COPIES,)),
        pltpu.SemaphoreType.DMA((BWD_COPIES,)),
        pltpu.SemaphoreType.DMA((BWD_LOCALS,)),
    ]
    anywhere = pl.BlockSpec(memory_space=pl.ANY)
    grad_shape = jax.ShapeDtypeStruct((NZ, HEADS, WROWS, HD), BF16)
    return pl.pallas_call(
        bwd_kernel,
        out_shape=[jax.ShapeDtypeStruct((ROWS, TOK, E), F32), grad_shape, grad_shape],
        in_specs=[pl.BlockSpec(memory_space=pltpu.SMEM)] + [anywhere] * (len(CHUNKS) + 2),
        out_specs=[pl.BlockSpec(memory_space=pltpu.VMEM), anywhere, anywhere],
        scratch_shapes=scratch,
        compiler_params=pltpu.CompilerParams(
            collective_id=1, has_side_effects=True, vmem_limit_bytes=VMEM_LIMIT
        ),
        name="sum_grads",
    )(meta, *terms, kgrad, vgrad)


def describe(nbr_shard, nbr_row):
    owners, rows = nbr_shard.reshape(SLOTS), nbr_row.reshape(SLOTS)
    entry = (owners // NY) * ROWS + rows
    column = lax.rem(owners, NY)
    slots = jnp.arange(SLOTS, dtype=jnp.int32)
    same = jnp.logical_and(owners[:, None] == owners[None, :], slots[:, None] > slots[None, :])
    key = owners * 2 + jnp.sum(same.astype(jnp.int32), axis=1)
    hit = key[:, None] == jnp.arange(128, dtype=jnp.int32)[None, :]
    slot_of = jnp.sum(jnp.where(hit, slots[:, None], 0), axis=0)
    row_of = jnp.sum(jnp.where(hit, rows[:, None] + 1, 0), axis=0) - 1
    pad = (0, 128 - SLOTS)
    blank = jnp.zeros((128,), jnp.int32)
    return jnp.stack([jnp.pad(entry, pad), jnp.pad(column, pad), slot_of, row_of] + [blank] * 4)


def unpack(grad):
    return grad.transpose(0, 2, 1, 3).reshape(E, LOCAL).astype(F32)


def body(queries, states, key_weight, value_weight, nbr_shard, nbr_row, out_grad):
    *rows, metas = forward(describe(nbr_shard, nbr_row), states)
    attended, query_grad, *rest = attend(queries, out_grad, key_weight, value_weight, rows)
    terms, kgrad, vgrad = rest[:-2], rest[-2], rest[-1]
    state_total, ktotal, vtotal = backward(metas, terms, kgrad, vgrad)
    return attended, query_grad, state_total, unpack(ktotal), unpack(vtotal)


def solution(mesh):
    placed = (
        P("dp", "mp"),
        P("dp", "mp", None),
        P(None, "mp"),
        P(None, "mp"),
        P("dp", None),
        P("dp", None),
        P("dp", "mp"),
    )
    return jax.shard_map(
        body,
        mesh=mesh,
        in_specs=placed,
        out_specs=(P("dp", "mp"), P("dp", "mp"), P("dp", "mp", None), P(None, "mp"), P(None, "mp")),
        check_vma=False,
    )
```

```python
import jax
import jax.numpy as jnp
from jax import lax
from jax.experimental import pallas as pl
from jax.experimental.pallas import tpu as pltpu
from jax.sharding import PartitionSpec as P

D = 4096
H = 32
HD = 128
NZ, NY, NX = 8, 4, 4
GROUPS = 8
SLOTS = 12
HALF = SLOTS // 2
ROWS = 8
TOK = 16
E = 896
VMEM_LIMIT = 56 * 1024 * 1024
BF16 = jnp.bfloat16
F32 = jnp.float32


class Place:
    def __init__(self):
        dp, mp = lax.axis_index("dp"), lax.axis_index("mp")
        self.dp, self.mp = dp, mp
        self.z, self.y = dp // NY, lax.rem(dp, NY)
        self.x, self.core = mp // 2, lax.rem(mp, 2)

    def zi(self, k):
        return lax.rem(self.z + (k + NZ), NZ)

    def yi(self, k):
        return lax.rem(self.y + (k + NY), NY)

    def xi(self, k):
        return lax.rem(self.x + (k + NX), NX)

    def at_z(self, k):
        return (self.zi(k) * NY + self.y, self.mp)

    def at_y(self, k):
        return (self.z * NY + self.yi(k), self.mp)

    def at_x(self, k):
        return (self.dp, self.xi(k) * 2 + self.core)

    def sibling(self):
        return (self.dp, self.x * 2 + (1 - self.core))

    def partners(self):
        return [
            self.at_z(1), self.at_z(-1), self.at_y(1), self.at_y(-1), self.at_y(2),
            self.at_x(1), self.at_x(-1), self.at_x(2), self.sibling(),
        ]


class Net:
    def __init__(self, send_sems, recv_sems, local_sems):
        self.send_sems, self.recv_sems, self.local_sems = send_sems, recv_sems, local_sems
        self.sent = []
        self.locals = 0

    def send(self, src, dst, device):
        number = len(self.sent)
        copy = pltpu.make_async_remote_copy(
            src_ref=src,
            dst_ref=dst,
            send_sem=self.send_sems.at[number],
            recv_sem=self.recv_sems.at[number],
            device_id=device,
            device_id_type=pl.DeviceIdType.MESH,
        )
        copy.start()
        self.sent.append(copy)
        return copy

    def local(self, src, dst):
        copy = pltpu.make_async_copy(src, dst, self.local_sems.at[self.locals])
        copy.start()
        self.locals += 1
        return copy

    def finish(self):
        for copy in self.sent:
            copy.wait_send()


def greet(place):
    barrier = pltpu.get_barrier_semaphore()
    partners = place.partners()
    for device in partners:
        pl.semaphore_signal(barrier, inc=1, device_id=device, device_id_type=pl.DeviceIdType.MESH)
    pl.semaphore_wait(barrier, len(partners))


def part(ref, bounds):
    first, count = bounds
    return ref.at[pl.ds(first, count)]


def ring_gather(net, n, right, left, slot, halves, landed=None):
    half_r, half_l = halves
    whole = (half_r[0], half_r[1] + half_l[1])
    far = n // 2
    for step in range(1, far + 1):
        piece_r = half_r if step == far else whole
        piece_l = half_l if step == far else whole
        block_r, block_l = part(slot(1 - step), piece_r), part(slot(step - 1), piece_l)
        to_right = net.send(block_r, block_r, right)
        to_left = net.send(block_l, block_l, left)
        yield
        to_right.wait_recv()
        if landed is not None:
            landed(part(slot(-step), piece_r))
        to_left.wait_recv()
        if landed is not None:
            landed(part(slot(step), piece_l))


def add_into(target, *others):
    total = target[...].astype(F32)
    for other in others:
        total = total + other[...].astype(F32)
    target[...] = total.astype(target.dtype)


def ring_scatter(net, n, right, left, total, prepare, from_left, from_right, halves):
    half_r, half_l = halves
    whole = (half_r[0], half_r[1] + half_l[1])
    far = n // 2
    prepare(far)
    to_right = [net.send(part(total(far), half_r), part(from_left(0), half_r), right)]
    to_left = [net.send(part(total(far), half_l), part(from_right(0), half_l), left)]
    for step in range(1, far):
        k = far - step
        prepare(k)
        prepare(-k)
        early_r, early_l = [], []
        if step == 1:
            early_r.append(net.send(part(total(k), half_l), part(from_left(step), half_l), right))
            early_l.append(net.send(part(total(-k), half_r), part(from_right(step), half_r), left))
        piece_r = half_r if step == 1 else whole
        piece_l = half_l if step == 1 else whole
        yield
        for copy in to_right:
            copy.wait_recv()
        add_into(part(total(k), piece_r), part(from_left(step - 1), piece_r))
        to_right = early_r + [net.send(part(total(k), piece_r), part(from_left(step), piece_r), right)]
        for copy in to_left:
            copy.wait_recv()
        add_into(part(total(-k), piece_l), part(from_right(step - 1), piece_l))
        to_left = early_l + [net.send(part(total(-k), piece_l), part(from_right(step), piece_l), left)]
    prepare(0)
    yield
    for copy in to_right + to_left:
        copy.wait_recv()
    add_into(total(0), from_left(far - 1), from_right(far - 1))


ROW_HALVES = ((0, ROWS // 2), (ROWS // 2, ROWS // 2))
SPAN_LEN = 64
LOCAL = 512
PARTS = 3
SPART = SLOTS // PARTS
PROWS = GROUPS * SPART * TOK
WROWS = E // NZ
UNITS = 4
UNIT_HALVES = ((0, UNITS // 2), (UNITS // 2, UNITS // 2))
ZBLOCK_HALVES = ((0, NZ // 2), (NZ // 2, NZ // 2))
WROW_HALVES = ((0, 64), (64, WROWS - 64))
COPIES = 160
LOCALS = 32
AROUND = (1, -1, 2)


def mm(a, b, dims):
    return lax.dot_general(a, b, (dims, ((), ())), preferred_element_type=F32)


def kernel(
    meta_in, states, queries, out_grad, key_weight, value_weight,
    att, qg, state_out, kout, vout,
    meta_v, meta_s, q, g, weights, zbuf, ysend, yrecv, rows, rows_t, grads, terms, theirs, xrecv,
    ybuf, share, zl, zr, wgrad, wfl, wfr, wy, wres, vyl, vyr, vzl, vzr, vres,
    send_sems, recv_sems, local_sems,
):
    place = Place()
    net = Net(send_sems, recv_sems, local_sems)
    y, mp = place.y, place.mp
    load_states = net.local(states, zbuf.at[place.z])
    own_meta = net.local(meta_in, meta_v.at[y])
    loads = []
    half = LOCAL // 2
    for i in range(2):
        from_cols = pl.ds(i * half, half)
        loads.append(net.local(key_weight.at[:, from_cols], weights.at[i, :, pl.ds(0, half)]))
        loads.append(net.local(value_weight.at[:, from_cols], weights.at[i, :, pl.ds(half, half)]))
    loads.append(net.local(queries, q))
    loads.append(net.local(out_grad, g))
    greet(place)

    meta_copies = [net.send(meta_in, meta_v.at[y], place.at_y(k)) for k in AROUND]
    load_states.wait()
    for turn, _ in enumerate(
        ring_gather(net, NZ, place.at_z(1), place.at_z(-1), lambda k: zbuf.at[place.zi(k)], ROW_HALVES)
    ):
        if turn == 1:
            own_meta.wait()
            for copy in meta_copies:
                copy.wait_recv()
            to_smem = net.local(meta_v, meta_s)
    to_smem.wait()

    def fetch(p):
        at = pl.ds(p * SPART, SPART)

        def held(k, j):
            entry = meta_s[place.yi(k), 0, j]
            return zbuf[entry // ROWS, lax.rem(entry, ROWS)]

        copies = []
        for n, k in enumerate(AROUND):
            for j in range(SPART):
                ysend[p, n, j] = held(k, p * SPART + j)
            copies.append(net.send(ysend.at[p, n], yrecv.at[p, n], place.at_y(k)))
        yield
        for copy in copies:
            copy.wait_recv()
        for j in range(SPART):
            column = meta_s[y, 1, p * SPART + j]
            value = lax.select(column == place.yi(-1), yrecv[p, 0, j], yrecv[p, 1, j])
            value = lax.select(column == place.yi(2), yrecv[p, 2, j], value)
            rows[mp, p * SPART + j] = lax.select(column == y, held(0, p * SPART + j), value)

        def block(k):
            return rows.at[place.xi(k) * 2 + place.core, at]

        across = [net.send(block(0), block(0), place.sibling())]
        copies = [net.send(block(0), block(0), place.at_x(k)) for k in AROUND]
        yield
        for copy, k in zip(copies, (-1, 1, 2)):
            copy.wait_recv()
            across.append(net.send(block(k), block(k), place.sibling()))
        yield
        for copy in across:
            copy.wait_recv()

    def attend(p, i):
        scale = 1.0 / HD**0.5
        at = pl.ds(p * SPART, SPART)
        part_rows = rows[:, at].reshape(PROWS, E)
        if i == 0:
            rows_t[:, pl.ds(p * PROWS, PROWS)] = part_rows.T
        both = mm(part_rows, weights[i], ((1,), (0,))).astype(BF16).reshape(GROUPS, SPART, TOK, LOCAL)
        for c in range(SPART // 2):
            span_both = both[:, 2 * c:2 * c + 2].reshape(2 * GROUPS * TOK, LOCAL)
            span = pl.ds((p * (SPART // 2) + c) * SPAN_LEN, SPAN_LEN)
            for h in range(2):
                cols = pl.ds((2 * i + h) * HD, HD)
                qh, gh = q[span, cols], g[span, cols]
                kh = span_both[:, h * HD:(h + 1) * HD]
                vh = span_both[:, half + h * HD:half + (h + 1) * HD]
                scores = mm(qh, kh, ((1,), (1,))) * scale
                top = jnp.max(scores, axis=-1, keepdims=True)
                grown = jnp.exp(scores - top)
                probs = grown / jnp.sum(grown, axis=-1, keepdims=True)
                low = probs.astype(BF16)
                att[span, cols] = mm(low, vh, ((1,), (0,))).astype(BF16)
                pgrad = mm(gh, vh, ((1,), (1,)))
                dot = jnp.sum(probs * pgrad, axis=-1, keepdims=True)
                sgrad = (scale * probs * (pgrad - dot)).astype(BF16)
                qg[span, cols] = mm(sgrad, kh, ((1,), (0,))).astype(BF16)
                shape = (GROUPS, 2, TOK, HD)
                pair = pl.ds(2 * c, 2)
                grads[i, p, :, pair, :, pl.ds(h * HD, HD)] = (
                    mm(sgrad, qh, ((0,), (0,))).astype(BF16).reshape(shape)
                )
                grads[i, p, :, pair, :, pl.ds(half + h * HD, HD)] = (
                    mm(low, gh, ((0,), (0,))).astype(BF16).reshape(shape)
                )

    def slab_term(p):
        total = None
        for i in range(2):
            term = mm(grads[i, p].reshape(PROWS, LOCAL), weights[i], ((1,), (1,)))
            total = term if total is None else total + term
        terms[:, pl.ds(p * SPART, SPART)] = total.astype(BF16).reshape(GROUPS, SPART, TOK, E)

    def weight_term(i):
        total = mm(rows_t[...], grads[i].reshape(PARTS * PROWS, LOCAL), ((1,), (0,))).astype(BF16)
        for z in range(NZ):
            for u in range(UNITS):
                wgrad[i, z, u] = total[z * WROWS:(z + 1) * WROWS, u * HD:(u + 1) * HD]

    def give_back(p):
        at = pl.ds(p * SPART, SPART)
        order = AROUND + (0,)
        copies = [
            net.send(terms.at[place.xi(k) * 2 + (1 - place.core), at], theirs.at[p, n], place.sibling())
            for n, k in enumerate(order)
        ]
        yield
        crossing = []
        for n, k in enumerate(order):
            copies[n].wait_recv()
            block = terms.at[place.xi(k) * 2 + place.core, at]
            add_into(block, theirs.at[p, n])
            if k != 0:
                crossing.append(net.send(block, xrecv.at[p, n], place.at_x(k)))
        yield
        for copy in crossing:
            copy.wait_recv()
        total = terms[mp, at].astype(F32)
        for n in range(3):
            total = total + xrecv[p, n].astype(F32)
        ybuf[y, at] = total.astype(BF16)
        copies = [net.send(ybuf.at[y, at], ybuf.at[y, at], place.at_y(k)) for k in AROUND]
        yield
        for copy in copies:
            copy.wait_recv()

    def nothing(k):
        pass

    def sum_slabs():
        def prepare(k):
            shard = place.zi(k) * NY + y
            named = [
                (d, meta_s[d, 2, shard * 2 + r], meta_s[d, 3, shard * 2 + r]) for d in range(NY) for r in range(2)
            ]
            for row in range(ROWS):
                total = None
                for d, slot, slot_row in named:
                    weight = jnp.where(slot_row == row, 1.0, 0.0).astype(F32)
                    term = ybuf[d, slot].astype(F32) * weight
                    total = term if total is None else total + term
                share[(k + NZ) % NZ, row] = total.astype(BF16)

        yield from ring_scatter(
            net, NZ, place.at_z(1), place.at_z(-1), lambda k: share.at[(k + NZ) % NZ], prepare,
            lambda s: zl.at[s], lambda s: zr.at[s], ROW_HALVES,
        )
        state_out[...] = share[0].astype(F32)

    def result(res, i):
        return [
            net.local(res.at[:, u], out.at[:, :, pl.ds((2 * i + u % 2) * HD, HD)])
            for u, out in enumerate((kout, kout, vout, vout))
        ]

    def sum_z_first():
        total = wgrad.at[0]
        yield from ring_scatter(
            net, NZ, place.at_z(1), place.at_z(-1), lambda k: total.at[place.zi(k)], nothing,
            lambda s: wfl.at[s], lambda s: wfr.at[s], UNIT_HALVES,
        )
        wy[y] = total[place.z]
        copies = [net.send(wy.at[y], wy.at[y], place.at_y(k)) for k in AROUND]
        yield
        for copy in copies:
            copy.wait_recv()
        whole = wy[0].astype(F32)
        for d in range(1, NY):
            whole = whole + wy[d].astype(F32)
        wres[place.z] = whole.astype(BF16)
        yield from ring_gather(
            net, NZ, place.at_z(1), place.at_z(-1), lambda k: wres.at[place.zi(k)], UNIT_HALVES
        )
        done = result(wres, 0)
        yield
        for copy in done:
            copy.wait()

    def sum_y_first():
        total = wgrad.at[1]
        yield from ring_scatter(
            net, NY, place.at_y(1), place.at_y(-1), lambda k: total.at[:, place.yi(k)], nothing,
            lambda s: vyl.at[s], lambda s: vyr.at[s], ZBLOCK_HALVES,
        )
        yield from ring_scatter(
            net, NZ, place.at_z(1), place.at_z(-1), lambda k: total.at[place.zi(k), y], nothing,
            lambda s: vzl.at[s], lambda s: vzr.at[s], WROW_HALVES,
        )
        vres[place.z, y] = total[place.z, y]
        yield from ring_gather(
            net, NZ, place.at_z(1), place.at_z(-1), lambda k: vres.at[place.zi(k), y], WROW_HALVES
        )
        yield from ring_gather(
            net, NY, place.at_y(1), place.at_y(-1), lambda k: vres.at[:, place.yi(k)], ZBLOCK_HALVES
        )
        done = result(vres, 1)
        yield
        for copy in done:
            copy.wait()

    def go(chain):
        return next(chain, chain) is not chain

    f = [fetch(p) for p in range(PARTS)]
    s = [give_back(p) for p in range(PARTS)]
    first, second = sum_z_first(), sum_y_first()
    go(f[0])
    go(f[0])
    go(f[1])
    go(f[0])
    go(f[1])
    go(f[2])
    go(f[0])
    for copy in loads:
        copy.wait()
    attend(0, 0)
    go(f[1])
    go(f[2])
    attend(0, 1)
    slab_term(0)
    go(s[0])
    go(f[1])
    attend(1, 0)
    go(f[2])
    go(s[0])
    attend(1, 1)
    slab_term(1)
    go(s[1])
    go(f[2])
    attend(2, 0)
    go(s[0])
    go(s[1])
    weight_term(0)
    go(first)
    attend(2, 1)
    slab_term(2)
    go(s[2])
    go(s[0])
    go(s[1])
    go(first)
    go(s[2])
    weight_term(1)
    go(second)
    go(s[1])
    go(first)
    go(s[2])
    go(second)
    go(first)
    go(s[2])
    slabs = sum_slabs()
    live = [slabs, second, first]
    while live:
        live = [chain for chain in live if go(chain)]
    net.finish()


def fused(meta, states, queries, out_grad, key_weight, value_weight):
    slab = (TOK, E)
    block = (WROWS, HD)
    scratch = [
        pltpu.VMEM((NY, 8, 128), jnp.int32),
        pltpu.SMEM((NY, 8, 128), jnp.int32),
        pltpu.VMEM(queries.shape, BF16),
        pltpu.VMEM(out_grad.shape, BF16),
        pltpu.VMEM((2, E, LOCAL), BF16),
        pltpu.VMEM((NZ, ROWS) + slab, BF16),
        pltpu.VMEM((PARTS, 3, SPART) + slab, BF16),
        pltpu.VMEM((PARTS, 3, SPART) + slab, BF16),
        pltpu.VMEM((GROUPS, SLOTS) + slab, BF16),
        pltpu.VMEM((E, PARTS * PROWS), BF16),
        pltpu.VMEM((2, PARTS, GROUPS, SPART, TOK, LOCAL), BF16),
        pltpu.VMEM((GROUPS, SLOTS) + slab, BF16),
        pltpu.VMEM((PARTS, NX, SPART) + slab, BF16),
        pltpu.VMEM((PARTS, 3, SPART) + slab, BF16),
        pltpu.VMEM((NY, SLOTS) + slab, BF16),
        pltpu.VMEM((NZ, ROWS) + slab, BF16),
        pltpu.VMEM((NZ // 2, ROWS) + slab, BF16),
        pltpu.VMEM((NZ // 2, ROWS) + slab, BF16),
        pltpu.VMEM((2, NZ, UNITS) + block, BF16),
        pltpu.VMEM((NZ // 2, UNITS) + block, BF16),
        pltpu.VMEM((NZ // 2, UNITS) + block, BF16),
        pltpu.VMEM((NY, UNITS) + block, BF16),
        pltpu.VMEM((NZ, UNITS) + block, BF16),
        pltpu.VMEM((NY // 2, NZ) + block, BF16),
        pltpu.VMEM((NY // 2, NZ) + block, BF16),
        pltpu.VMEM((NZ // 2,) + block, BF16),
        pltpu.VMEM((NZ // 2,) + block, BF16),
        pltpu.VMEM((NZ, UNITS) + block, BF16),
        pltpu.SemaphoreType.DMA((COPIES,)),
        pltpu.SemaphoreType.DMA((COPIES,)),
        pltpu.SemaphoreType.DMA((LOCALS,)),
    ]
    anywhere = pl.BlockSpec(memory_space=pl.ANY)
    vmem = pl.BlockSpec(memory_space=pltpu.VMEM)
    wshape = jax.ShapeDtypeStruct((NZ, WROWS, LOCAL), BF16)
    return pl.pallas_call(
        kernel,
        out_shape=[
            jax.ShapeDtypeStruct(queries.shape, BF16),
            jax.ShapeDtypeStruct(queries.shape, BF16),
            jax.ShapeDtypeStruct(states.shape, F32),
            wshape,
            wshape,
        ],
        in_specs=[vmem] + [anywhere] * 5,
        out_specs=[vmem] * 3 + [anywhere] * 2,
        scratch_shapes=scratch,
        compiler_params=pltpu.CompilerParams(
            collective_id=0, has_side_effects=True, vmem_limit_bytes=VMEM_LIMIT
        ),
        name="retrieve",
    )(meta, states, queries, out_grad, key_weight, value_weight)


def describe(nbr_shard, nbr_row):
    spans, count = nbr_shard.shape
    slots = jnp.arange(SLOTS, dtype=jnp.int32)
    spot = jnp.arange(count, dtype=jnp.int32)[:, None] + count * jnp.arange(spans, dtype=jnp.int32)[None, :]
    pick = (spot[:, :, None] == slots[None, None, :]).astype(jnp.int32)
    owners = jnp.sum(nbr_shard.T[:, :, None] * pick, axis=(0, 1))
    rows = jnp.sum(nbr_row.T[:, :, None] * pick, axis=(0, 1))
    entry = (owners // NY) * ROWS + rows
    column = lax.rem(owners, NY)
    same = jnp.logical_and(owners[:, None] == owners[None, :], slots[:, None] > slots[None, :])
    key = owners * 2 + jnp.sum(same.astype(jnp.int32), axis=1)
    hit = key[:, None] == jnp.arange(128, dtype=jnp.int32)[None, :]
    slot_of = jnp.sum(jnp.where(hit, slots[:, None], 0), axis=0)
    row_of = jnp.sum(jnp.where(hit, rows[:, None] + 1, 0), axis=0) - 1
    pad = (0, 128 - SLOTS)
    blank = jnp.zeros((128,), jnp.int32)
    return jnp.stack([jnp.pad(entry, pad), jnp.pad(column, pad), slot_of, row_of] + [blank] * 4)


def body(queries, states, key_weight, value_weight, nbr_shard, nbr_row, out_grad):
    attended, query_grad, state_total, ktotal, vtotal = fused(
        describe(nbr_shard, nbr_row), states, queries, out_grad, key_weight, value_weight
    )
    return (
        attended, query_grad, state_total,
        ktotal.reshape(E, LOCAL).astype(F32), vtotal.reshape(E, LOCAL).astype(F32),
    )


def solution(mesh):
    placed = (
        P("dp", "mp"),
        P("dp", "mp", None),
        P(None, "mp"),
        P(None, "mp"),
        P("dp", None),
        P("dp", None),
        P("dp", "mp"),
    )
    return jax.shard_map(
        body,
        mesh=mesh,
        in_specs=placed,
        out_specs=(P("dp", "mp"), P("dp", "mp"), P("dp", "mp", None), P(None, "mp"), P(None, "mp")),
        check_vma=False,
    )
```

```python
import functools

import jax
import jax.numpy as jnp
from jax import lax
from jax.experimental import pallas as pl
from jax.experimental.pallas import tpu as pltpu
from jax.sharding import PartitionSpec as P

D = 4096
H = 32
HD = 128
NZ, NY, NX = 8, 4, 4
GROUPS = 8
SLOTS = 12
HALF = SLOTS // 2
ROWS = 8
TOK = 16
E = 896
VMEM_LIMIT = 56 * 1024 * 1024
BF16 = jnp.bfloat16
F32 = jnp.float32


class Place:
    def __init__(self):
        dp, mp = lax.axis_index("dp"), lax.axis_index("mp")
        self.dp, self.mp = dp, mp
        self.z, self.y = dp // NY, lax.rem(dp, NY)
        self.x, self.core = mp // 2, lax.rem(mp, 2)

    def zi(self, k):
        return lax.rem(self.z + (k + NZ), NZ)

    def yi(self, k):
        return lax.rem(self.y + (k + NY), NY)

    def xi(self, k):
        return lax.rem(self.x + (k + NX), NX)

    def at_z(self, k):
        return (self.zi(k) * NY + self.y, self.mp)

    def at_y(self, k):
        return (self.z * NY + self.yi(k), self.mp)

    def at_x(self, k):
        return (self.dp, self.xi(k) * 2 + self.core)

    def sibling(self):
        return (self.dp, self.x * 2 + (1 - self.core))

    def partners(self):
        return [
            self.at_z(1), self.at_z(-1), self.at_y(1), self.at_y(-1), self.at_y(2),
            self.at_x(1), self.at_x(-1), self.at_x(2), self.sibling(),
        ]


class Net:
    def __init__(self, send_sems, recv_sems, local_sems):
        self.send_sems, self.recv_sems, self.local_sems = send_sems, recv_sems, local_sems
        self.sent = []
        self.locals = 0

    def send(self, src, dst, device):
        number = len(self.sent)
        copy = pltpu.make_async_remote_copy(
            src_ref=src,
            dst_ref=dst,
            send_sem=self.send_sems.at[number],
            recv_sem=self.recv_sems.at[number],
            device_id=device,
            device_id_type=pl.DeviceIdType.MESH,
        )
        copy.start()
        self.sent.append(copy)
        return copy

    def local(self, src, dst):
        copy = pltpu.make_async_copy(src, dst, self.local_sems.at[self.locals])
        copy.start()
        self.locals += 1
        return copy

    def finish(self):
        for copy in self.sent:
            copy.wait_send()


def greet(place):
    barrier = pltpu.get_barrier_semaphore()
    partners = place.partners()
    for device in partners:
        pl.semaphore_signal(barrier, inc=1, device_id=device, device_id_type=pl.DeviceIdType.MESH)
    pl.semaphore_wait(barrier, len(partners))


def part(ref, bounds):
    first, count = bounds
    return ref.at[pl.ds(first, count)]


def ring_gather(net, n, right, left, slot, halves, landed=None):
    half_r, half_l = halves
    whole = (half_r[0], half_r[1] + half_l[1])
    far = n // 2
    for step in range(1, far + 1):
        piece_r = half_r if step == far else whole
        piece_l = half_l if step == far else whole
        block_r, block_l = part(slot(1 - step), piece_r), part(slot(step - 1), piece_l)
        to_right = net.send(block_r, block_r, right)
        to_left = net.send(block_l, block_l, left)
        yield
        to_right.wait_recv()
        if landed is not None:
            landed(part(slot(-step), piece_r))
        to_left.wait_recv()
        if landed is not None:
            landed(part(slot(step), piece_l))


def add_into(target, *others):
    total = target[...].astype(F32)
    for other in others:
        total = total + other[...].astype(F32)
    target[...] = total.astype(target.dtype)


def ring_scatter(net, n, right, left, total, prepare, from_left, from_right, halves):
    half_r, half_l = halves
    whole = (half_r[0], half_r[1] + half_l[1])
    far = n // 2
    prepare(far)
    to_right = [net.send(part(total(far), half_r), part(from_left(0), half_r), right)]
    to_left = [net.send(part(total(far), half_l), part(from_right(0), half_l), left)]
    for step in range(1, far):
        k = far - step
        prepare(k)
        prepare(-k)
        early_r, early_l = [], []
        if step == 1:
            early_r.append(net.send(part(total(k), half_l), part(from_left(step), half_l), right))
            early_l.append(net.send(part(total(-k), half_r), part(from_right(step), half_r), left))
        piece_r = half_r if step == 1 else whole
        piece_l = half_l if step == 1 else whole
        yield
        for copy in to_right:
            copy.wait_recv()
        add_into(part(total(k), piece_r), part(from_left(step - 1), piece_r))
        to_right = early_r + [net.send(part(total(k), piece_r), part(from_left(step), piece_r), right)]
        for copy in to_left:
            copy.wait_recv()
        add_into(part(total(-k), piece_l), part(from_right(step - 1), piece_l))
        to_left = early_l + [net.send(part(total(-k), piece_l), part(from_right(step), piece_l), left)]
    prepare(0)
    yield
    for copy in to_right + to_left:
        copy.wait_recv()
    add_into(total(0), from_left(far - 1), from_right(far - 1))


ROW_HALVES = ((0, ROWS // 2), (ROWS // 2, ROWS // 2))
SPAN_LEN = 64
LOCAL = 512
NLEN = GROUPS * TOK
PARTS = ((0, 4), (4, 4), (8, 4))
WROWS = E // NZ
UNITS = 4
Y_FIRST = 1
UNIT_HALVES = ((0, UNITS // 2), (UNITS // 2, UNITS // 2))
ZBLOCK_HALVES = ((0, NZ // 2), (NZ // 2, NZ // 2))
WROW_HALVES = ((0, 64), (64, WROWS - 64))
COPIES = 160
LOCALS = 32
AROUND = (1, -1, 2)
PLAN = (
    "f0", "load", "f1", "f2", "f0", "f1", "f0", "f2", "f0", "a00", "a01", "f1", "f2", "t0", "f1", "a10", "f2",
    "a20", "w0", "B", "a21", "s0", "a11", "s0", "B", "t1", "s1", "w1", "A", "s1", "B", "t2", "s2", "s0", "A",
    "s2", "B", "s1", "B", "A", "s0", "B", "s2", "A", "B", "s1", "A", "B", "s2", "Z", "B", "A", "Z", "B", "A",
    "Z", "B", "A", "Z", "B", "A", "B", "B", "Z", "A", "A",
)


def mm(a, b, dims):
    return lax.dot_general(a, b, (dims, ((), ())), preferred_element_type=F32)


def kernel(
    meta_in, states, queries, out_grad, key_weight, value_weight,
    att, qg, state_out, kout, vout,
    meta_v, meta_s, q, g, weights, zbuf, ysend, yrecv, rows, rows_t, grads, terms, theirs, xrecv,
    ybuf, share, zl, zr, wgrad, wfl, wfr, wy, wres, vyl, vyr, vzl, vzr, vres, wide,
    send_sems, recv_sems, local_sems,
):
    place = Place()
    net = Net(send_sems, recv_sems, local_sems)
    y, mp = place.y, place.mp
    load_states = net.local(states, zbuf.at[place.z])
    own_meta = net.local(meta_in, meta_v.at[y])
    loads = []
    half = LOCAL // 2
    for i in range(2):
        from_cols = pl.ds(i * half, half)
        loads.append(net.local(key_weight.at[:, from_cols], weights.at[i, :, pl.ds(0, half)]))
        loads.append(net.local(value_weight.at[:, from_cols], weights.at[i, :, pl.ds(half, half)]))
    loads.append(net.local(queries, q))
    loads.append(net.local(out_grad, g))
    greet(place)

    meta_copies = [net.send(meta_in, meta_v.at[y], place.at_y(k)) for k in AROUND]
    load_states.wait()
    for turn, _ in enumerate(
        ring_gather(net, NZ, place.at_z(1), place.at_z(-1), lambda k: zbuf.at[place.zi(k)], ROW_HALVES)
    ):
        if turn == 1:
            own_meta.wait()
            for copy in meta_copies:
                copy.wait_recv()
            to_smem = net.local(meta_v, meta_s)
    to_smem.wait()

    def fetch(p):
        first, count = PARTS[p]
        at = pl.ds(first, count)
        slots = range(first, first + count)

        def held(k, j):
            entry = meta_s[place.yi(k), 0, j]
            return zbuf[entry // ROWS, lax.rem(entry, ROWS)]

        copies = []
        for n, k in enumerate(AROUND):
            for j in slots:
                ysend[n, j] = held(k, j)
            copies.append(net.send(ysend.at[n, at], yrecv.at[n, at], place.at_y(k)))
        yield
        for copy in copies:
            copy.wait_recv()
        for j in slots:
            column = meta_s[y, 1, j]
            value = lax.select(column == place.yi(-1), yrecv[0, j], yrecv[1, j])
            value = lax.select(column == place.yi(2), yrecv[2, j], value)
            rows[mp, j] = lax.select(column == y, held(0, j), value)

        def block(k):
            return rows.at[place.xi(k) * 2 + place.core, at]

        across = [net.send(block(0), block(0), place.sibling())]
        copies = [net.send(block(0), block(0), place.at_x(k)) for k in AROUND]
        yield
        for copy, k in zip(copies, (-1, 1, 2)):
            copy.wait_recv()
            across.append(net.send(block(k), block(k), place.sibling()))
        yield
        for copy in across:
            copy.wait_recv()

    def attend(p, i):
        scale = 1.0 / HD**0.5
        first, count = PARTS[p]
        part_rows = jnp.concatenate([rows[:, j].reshape(NLEN, E) for j in range(first, first + count)], axis=0)
        if i == Y_FIRST:
            rows_t[:, pl.ds(first * NLEN, count * NLEN)] = part_rows.T
        both = mm(part_rows, weights[i], ((1,), (0,))).astype(BF16)
        for c in range(count // 2):
            span_both = both[2 * c * NLEN:2 * (c + 1) * NLEN]
            span = pl.ds((first // 2 + c) * SPAN_LEN, SPAN_LEN)
            span_rows = pl.ds((first + 2 * c) * NLEN, 2 * NLEN)
            for h in range(2):
                cols = pl.ds((2 * i + h) * HD, HD)
                qh, gh = q[span, cols], g[span, cols]
                kh = span_both[:, h * HD:(h + 1) * HD]
                vh = span_both[:, half + h * HD:half + (h + 1) * HD]
                scores = mm(qh, kh, ((1,), (1,))) * scale
                top = jnp.max(scores, axis=-1, keepdims=True)
                grown = jnp.exp(scores - top)
                probs = grown / jnp.sum(grown, axis=-1, keepdims=True)
                low = probs.astype(BF16)
                att[span, cols] = mm(low, vh, ((1,), (0,))).astype(BF16)
                pgrad = mm(gh, vh, ((1,), (1,)))
                dot = jnp.sum(probs * pgrad, axis=-1, keepdims=True)
                sgrad = (scale * probs * (pgrad - dot)).astype(BF16)
                qg[span, cols] = mm(sgrad, kh, ((1,), (0,))).astype(BF16)
                grads[i, span_rows, pl.ds(h * HD, HD)] = mm(sgrad, qh, ((0,), (0,))).astype(BF16)
                grads[i, span_rows, pl.ds(half + h * HD, HD)] = mm(low, gh, ((0,), (0,))).astype(BF16)

    def slab_term(p):
        first, count = PARTS[p]
        total = None
        for i in range(2):
            term = mm(grads[i, pl.ds(first * NLEN, count * NLEN)], weights[i], ((1,), (1,)))
            total = term if total is None else total + term
        total = total.astype(BF16)
        for j in range(count):
            terms[:, first + j] = total[j * NLEN:(j + 1) * NLEN].reshape(GROUPS, TOK, E)

    def weight_term(i):
        total = mm(rows_t[...], grads[i], ((1,), (0,))).astype(BF16)
        for z in range(NZ):
            for u in range(UNITS):
                wgrad[i, z, u] = total[z * WROWS:(z + 1) * WROWS, u * HD:(u + 1) * HD]

    def give_back(p):
        at = pl.ds(*PARTS[p])
        order = AROUND + (0,)
        copies = [
            net.send(terms.at[place.xi(k) * 2 + (1 - place.core), at], theirs.at[n, at], place.sibling())
            for n, k in enumerate(order)
        ]
        yield
        crossing = []
        for n, k in enumerate(order):
            copies[n].wait_recv()
            block = terms.at[place.xi(k) * 2 + place.core, at]
            add_into(block, theirs.at[n, at])
            if k != 0:
                crossing.append(net.send(block, xrecv.at[n, at], place.at_x(k)))
        yield
        for copy in crossing:
            copy.wait_recv()
        total = terms[mp, at].astype(F32)
        for n in range(3):
            total = total + xrecv[n, at].astype(F32)
        ybuf[y, at] = total.astype(BF16)
        copies = [net.send(ybuf.at[y, at], ybuf.at[y, at], place.at_y(k)) for k in AROUND]
        yield
        for copy in copies:
            copy.wait_recv()

    def nothing(k):
        pass

    def sum_slabs():
        def prepare(k):
            shard = place.zi(k) * NY + y
            named = [
                (d, meta_s[d, 2, shard * 2 + r], meta_s[d, 3, shard * 2 + r]) for d in range(NY) for r in range(2)
            ]
            for row in range(ROWS):
                total = None
                for d, slot, slot_row in named:
                    weight = jnp.where(slot_row == row, 1.0, 0.0).astype(F32)
                    term = ybuf[d, slot].astype(F32) * weight
                    total = term if total is None else total + term
                share[(k + NZ) % NZ, row] = total.astype(BF16)

        yield from ring_scatter(
            net, NZ, place.at_z(1), place.at_z(-1), lambda k: share.at[(k + NZ) % NZ], prepare,
            lambda s: zl.at[s], lambda s: zr.at[s], ROW_HALVES,
        )
        state_out[...] = share[0].astype(F32)

    def result(res, i):
        copies = []
        for u, out in enumerate((kout, kout, vout, vout)):
            wide[i, u] = res[:, u].astype(F32)
            copies.append(net.local(wide.at[i, u], out.at[:, :, pl.ds((2 * i + u % 2) * HD, HD)]))
        return copies

    def sum_z_first():
        total = wgrad.at[0]
        yield from ring_scatter(
            net, NZ, place.at_z(1), place.at_z(-1), lambda k: total.at[place.zi(k)], nothing,
            lambda s: wfl.at[s], lambda s: wfr.at[s], UNIT_HALVES,
        )
        wy[y] = total[place.z]
        copies = [net.send(wy.at[y], wy.at[y], place.at_y(k)) for k in AROUND]
        yield
        for copy in copies:
            copy.wait_recv()
        whole = wy[0].astype(F32)
        for d in range(1, NY):
            whole = whole + wy[d].astype(F32)
        wres[place.z] = whole.astype(BF16)
        yield from ring_gather(
            net, NZ, place.at_z(1), place.at_z(-1), lambda k: wres.at[place.zi(k)], UNIT_HALVES
        )
        done = result(wres, 0)
        yield
        for copy in done:
            copy.wait()

    def sum_y_first():
        total = wgrad.at[1]
        yield from ring_scatter(
            net, NY, place.at_y(1), place.at_y(-1), lambda k: total.at[:, place.yi(k)], nothing,
            lambda s: vyl.at[s], lambda s: vyr.at[s], ZBLOCK_HALVES,
        )
        yield from ring_scatter(
            net, NZ, place.at_z(1), place.at_z(-1), lambda k: total.at[place.zi(k), y], nothing,
            lambda s: vzl.at[s], lambda s: vzr.at[s], WROW_HALVES,
        )
        vres[place.z, y] = total[place.z, y]
        yield from ring_gather(
            net, NZ, place.at_z(1), place.at_z(-1), lambda k: vres.at[place.zi(k), y], WROW_HALVES
        )
        yield from ring_gather(
            net, NY, place.at_y(1), place.at_y(-1), lambda k: vres.at[:, place.yi(k)], ZBLOCK_HALVES
        )
        done = result(vres, 1)
        yield
        for copy in done:
            copy.wait()

    chains = {"A": sum_z_first(), "B": sum_y_first(), "Z": sum_slabs()}

    def load():
        for copy in loads:
            copy.wait()

    work = {"load": load, "w0": lambda: weight_term(Y_FIRST), "w1": lambda: weight_term(1 - Y_FIRST)}
    for p in range(len(PARTS)):
        chains[f"f{p}"] = fetch(p)
        chains[f"s{p}"] = give_back(p)
        work[f"t{p}"] = functools.partial(slab_term, p)
        work[f"a{p}0"] = functools.partial(attend, p, Y_FIRST)
        work[f"a{p}1"] = functools.partial(attend, p, 1 - Y_FIRST)
    for name in PLAN:
        if name in work:
            work[name]()
        else:
            next(chains[name], None)
    for chain in chains.values():
        for _ in chain:
            pass
    net.finish()


def fused(meta, states, queries, out_grad, key_weight, value_weight):
    slab = (TOK, E)
    block = (WROWS, HD)
    scratch = [
        pltpu.VMEM((NY, 8, 128), jnp.int32),
        pltpu.SMEM((NY, 8, 128), jnp.int32),
        pltpu.VMEM(queries.shape, BF16),
        pltpu.VMEM(out_grad.shape, BF16),
        pltpu.VMEM((2, E, LOCAL), BF16),
        pltpu.VMEM((NZ, ROWS) + slab, BF16),
        pltpu.VMEM((len(AROUND), SLOTS) + slab, BF16),
        pltpu.VMEM((len(AROUND), SLOTS) + slab, BF16),
        pltpu.VMEM((GROUPS, SLOTS) + slab, BF16),
        pltpu.VMEM((E, SLOTS * NLEN), BF16),
        pltpu.VMEM((2, SLOTS * NLEN, LOCAL), BF16),
        pltpu.VMEM((GROUPS, SLOTS) + slab, BF16),
        pltpu.VMEM((NX, SLOTS) + slab, BF16),
        pltpu.VMEM((len(AROUND), SLOTS) + slab, BF16),
        pltpu.VMEM((NY, SLOTS) + slab, BF16),
        pltpu.VMEM((NZ, ROWS) + slab, BF16),
        pltpu.VMEM((NZ // 2, ROWS) + slab, BF16),
        pltpu.VMEM((NZ // 2, ROWS) + slab, BF16),
        pltpu.VMEM((2, NZ, UNITS) + block, BF16),
        pltpu.VMEM((NZ // 2, UNITS) + block, BF16),
        pltpu.VMEM((NZ // 2, UNITS) + block, BF16),
        pltpu.VMEM((NY, UNITS) + block, BF16),
        pltpu.VMEM((NZ, UNITS) + block, BF16),
        pltpu.VMEM((NY // 2, NZ) + block, BF16),
        pltpu.VMEM((NY // 2, NZ) + block, BF16),
        pltpu.VMEM((NZ // 2,) + block, BF16),
        pltpu.VMEM((NZ // 2,) + block, BF16),
        pltpu.VMEM((NZ, UNITS) + block, BF16),
        pltpu.VMEM((2, UNITS, NZ) + block, F32),
        pltpu.SemaphoreType.DMA((COPIES,)),
        pltpu.SemaphoreType.DMA((COPIES,)),
        pltpu.SemaphoreType.DMA((LOCALS,)),
    ]
    anywhere = pl.BlockSpec(memory_space=pl.ANY)
    vmem = pl.BlockSpec(memory_space=pltpu.VMEM)
    wshape = jax.ShapeDtypeStruct((NZ, WROWS, LOCAL), F32)
    return pl.pallas_call(
        kernel,
        out_shape=[
            jax.ShapeDtypeStruct(queries.shape, BF16),
            jax.ShapeDtypeStruct(queries.shape, BF16),
            jax.ShapeDtypeStruct(states.shape, F32),
            wshape,
            wshape,
        ],
        in_specs=[vmem] + [anywhere] * 5,
        out_specs=[vmem] * 3 + [anywhere] * 2,
        scratch_shapes=scratch,
        compiler_params=pltpu.CompilerParams(
            collective_id=0, has_side_effects=True, vmem_limit_bytes=VMEM_LIMIT
        ),
        name="retrieve",
    )(meta, states, queries, out_grad, key_weight, value_weight)


def describe(nbr_shard, nbr_row):
    spans, count = nbr_shard.shape
    slots = jnp.arange(SLOTS, dtype=jnp.int32)
    spot = jnp.arange(count, dtype=jnp.int32)[:, None] + count * jnp.arange(spans, dtype=jnp.int32)[None, :]
    pick = (spot[:, :, None] == slots[None, None, :]).astype(jnp.int32)
    owners = jnp.sum(nbr_shard.T[:, :, None] * pick, axis=(0, 1))
    rows = jnp.sum(nbr_row.T[:, :, None] * pick, axis=(0, 1))
    entry = (owners // NY) * ROWS + rows
    column = lax.rem(owners, NY)
    same = jnp.logical_and(owners[:, None] == owners[None, :], slots[:, None] > slots[None, :])
    key = owners * 2 + jnp.sum(same.astype(jnp.int32), axis=1)
    hit = key[:, None] == jnp.arange(128, dtype=jnp.int32)[None, :]
    slot_of = jnp.sum(jnp.where(hit, slots[:, None], 0), axis=0)
    row_of = jnp.sum(jnp.where(hit, rows[:, None] + 1, 0), axis=0) - 1
    pad = (0, 128 - SLOTS)
    blank = jnp.zeros((128,), jnp.int32)
    return jnp.stack([jnp.pad(entry, pad), jnp.pad(column, pad), slot_of, row_of] + [blank] * 4)


def body(queries, states, key_weight, value_weight, nbr_shard, nbr_row, out_grad):
    attended, query_grad, state_total, ktotal, vtotal = fused(
        describe(nbr_shard, nbr_row), states, queries, out_grad, key_weight, value_weight
    )
    return (
        attended, query_grad, state_total,
        ktotal.reshape(E, LOCAL), vtotal.reshape(E, LOCAL),
    )


def solution(mesh):
    placed = (
        P("dp", "mp"),
        P("dp", "mp", None),
        P(None, "mp"),
        P(None, "mp"),
        P("dp", None),
        P("dp", None),
        P("dp", "mp"),
    )
    return jax.shard_map(
        body,
        mesh=mesh,
        in_specs=placed,
        out_specs=(P("dp", "mp"), P("dp", "mp"), P("dp", "mp", None), P(None, "mp"), P(None, "mp")),
        check_vma=False,
    )
```

```python
import functools

import jax
import jax.numpy as jnp
from jax import lax
from jax.experimental import pallas as pl
from jax.experimental.pallas import tpu as pltpu
from jax.sharding import PartitionSpec as P

D = 4096
H = 32
HD = 128
NZ, NY, NX = 8, 4, 4
GROUPS = 8
SLOTS = 12
HALF = SLOTS // 2
ROWS = 8
TOK = 16
E = 896
VMEM_LIMIT = 56 * 1024 * 1024
FINISH_STEPS = 4
BF16 = jnp.bfloat16
F32 = jnp.float32


class Place:
    def __init__(self):
        dp, mp = lax.axis_index("dp"), lax.axis_index("mp")
        self.dp, self.mp = dp, mp
        self.z, self.y = dp // NY, lax.rem(dp, NY)
        self.x, self.core = mp // 2, lax.rem(mp, 2)

    def zi(self, k):
        return lax.rem(self.z + (k + NZ), NZ)

    def yi(self, k):
        return lax.rem(self.y + (k + NY), NY)

    def xi(self, k):
        return lax.rem(self.x + (k + NX), NX)

    def at_z(self, k):
        return (self.zi(k) * NY + self.y, self.mp)

    def at_y(self, k):
        return (self.z * NY + self.yi(k), self.mp)

    def at_x(self, k):
        return (self.dp, self.xi(k) * 2 + self.core)

    def sibling(self):
        return (self.dp, self.x * 2 + (1 - self.core))

    def partners(self):
        return [
            self.at_z(1), self.at_z(-1), self.at_y(1), self.at_y(-1), self.at_y(2),
            self.at_x(1), self.at_x(-1), self.at_x(2), self.sibling(),
        ]


class Net:
    def __init__(self, send_sems, recv_sems, local_sems):
        self.send_sems, self.recv_sems, self.local_sems = send_sems, recv_sems, local_sems
        self.sent = []
        self.locals = 0

    def send(self, src, dst, device):
        number = len(self.sent)
        copy = pltpu.make_async_remote_copy(
            src_ref=src,
            dst_ref=dst,
            send_sem=self.send_sems.at[number],
            recv_sem=self.recv_sems.at[number],
            device_id=device,
            device_id_type=pl.DeviceIdType.MESH,
        )
        copy.start()
        self.sent.append(copy)
        return copy

    def local(self, src, dst):
        copy = pltpu.make_async_copy(src, dst, self.local_sems.at[self.locals])
        copy.start()
        self.locals += 1
        return copy

    def finish(self):
        for copy in self.sent:
            copy.wait_send()


def greet(place):
    barrier = pltpu.get_barrier_semaphore()
    partners = place.partners()
    for device in partners:
        pl.semaphore_signal(barrier, inc=1, device_id=device, device_id_type=pl.DeviceIdType.MESH)
    pl.semaphore_wait(barrier, len(partners))


def part(ref, bounds):
    first, count = bounds
    return ref.at[pl.ds(first, count)]


def ring_gather(net, n, right, left, slot, halves, landed=None):
    half_r, half_l = halves
    whole = (half_r[0], half_r[1] + half_l[1])
    far = n // 2
    for step in range(1, far + 1):
        piece_r = half_r if step == far else whole
        piece_l = half_l if step == far else whole
        block_r, block_l = part(slot(1 - step), piece_r), part(slot(step - 1), piece_l)
        to_right = net.send(block_r, block_r, right)
        to_left = net.send(block_l, block_l, left)
        yield
        to_right.wait_recv()
        if landed is not None:
            landed(part(slot(-step), piece_r))
        to_left.wait_recv()
        if landed is not None:
            landed(part(slot(step), piece_l))


def add_into(target, *others):
    total = target[...].astype(F32)
    for other in others:
        total = total + other[...].astype(F32)
    target[...] = total.astype(target.dtype)


def ring_scatter(net, n, right, left, total, prepare, from_left, from_right, halves):
    half_r, half_l = halves
    whole = (half_r[0], half_r[1] + half_l[1])
    far = n // 2
    prepare(far)
    to_right = [net.send(part(total(far), half_r), part(from_left(0), half_r), right)]
    to_left = [net.send(part(total(far), half_l), part(from_right(0), half_l), left)]
    for step in range(1, far):
        k = far - step
        prepare(k)
        prepare(-k)
        early_r, early_l = [], []
        if step == 1:
            early_r.append(net.send(part(total(k), half_l), part(from_left(step), half_l), right))
            early_l.append(net.send(part(total(-k), half_r), part(from_right(step), half_r), left))
        piece_r = half_r if step == 1 else whole
        piece_l = half_l if step == 1 else whole
        yield
        for copy in to_right:
            copy.wait_recv()
        add_into(part(total(k), piece_r), part(from_left(step - 1), piece_r))
        to_right = early_r + [net.send(part(total(k), piece_r), part(from_left(step), piece_r), right)]
        for copy in to_left:
            copy.wait_recv()
        add_into(part(total(-k), piece_l), part(from_right(step - 1), piece_l))
        to_left = early_l + [net.send(part(total(-k), piece_l), part(from_right(step), piece_l), left)]
    prepare(0)
    yield
    for copy in to_right + to_left:
        copy.wait_recv()
    add_into(total(0), from_left(far - 1), from_right(far - 1))


ROW_HALVES = ((0, ROWS // 2), (ROWS // 2, ROWS // 2))
SPAN_LEN = 64
LOCAL = 512
NLEN = GROUPS * TOK
PARTS = ((0, 4), (4, 4), (8, 2), (10, 2))
WROWS = E // NZ
UNITS = 4
Y_FIRST = 1
UNIT_HALVES = ((0, UNITS // 2), (UNITS // 2, UNITS // 2))
ZBLOCK_HALVES = ((0, NZ // 2), (NZ // 2, NZ // 2))
WROW_HALVES = ((0, 64), (64, WROWS - 64))
COPIES = 160
LOCALS = 32
AROUND = (1, -1, 2)
PLAN = (
    "f2", "f3", "load", "f1", "f2", "f3", "f0", "f2", "f1", "f2", "a20", "f3", "a21", "t2", "f3", "s2", "f0",
    "a30", "s2", "f1", "a31", "f1", "a10", "f0", "a11", "t1", "f0", "a00", "s1", "w0", "B", "s1", "a01", "w1",
    "A", "t3", "s3", "B", "t0", "s0", "s3", "s1", "s2", "A", "s0", "B", "A", "s3", "B", "s0", "s1", "B", "A",
    "B", "s2", "A", "s3", "B", "s0", "Z", "B", "A", "B", "Z", "B", "A", "Z", "B", "A", "Z", "B", "A", "B",
    "B", "Z", "A", "A",
)


def mm(a, b, dims):
    return lax.dot_general(a, b, (dims, ((), ())), preferred_element_type=F32)


def kernel(
    meta_in, states, queries, out_grad, key_weight, value_weight,
    att, qg, state_out, kout, vout,
    meta_v, meta_s, q, g, weights, zbuf, ysend, yrecv, rows, rows_t, grads, terms, theirs, xrecv,
    ybuf, share, zl, zr, wgrad, wfl, wfr, wy, wres, vyl, vyr, vzl, vzr, vres,
    send_sems, recv_sems, local_sems,
):
    place = Place()
    net = Net(send_sems, recv_sems, local_sems)
    y, mp = place.y, place.mp
    load_states = net.local(states, zbuf.at[place.z])
    own_meta = net.local(meta_in, meta_v.at[y])
    loads = []
    half = LOCAL // 2
    for i in range(2):
        from_cols = pl.ds(i * half, half)
        loads.append(net.local(key_weight.at[:, from_cols], weights.at[i, :, pl.ds(0, half)]))
        loads.append(net.local(value_weight.at[:, from_cols], weights.at[i, :, pl.ds(half, half)]))
    loads.append(net.local(queries, q))
    loads.append(net.local(out_grad, g))
    greet(place)

    meta_copies = [net.send(meta_in, meta_v.at[y], place.at_y(k)) for k in AROUND]
    load_states.wait()
    for turn, _ in enumerate(
        ring_gather(net, NZ, place.at_z(1), place.at_z(-1), lambda k: zbuf.at[place.zi(k)], ROW_HALVES)
    ):
        if turn == 1:
            own_meta.wait()
            for copy in meta_copies:
                copy.wait_recv()
            to_smem = net.local(meta_v, meta_s)
    to_smem.wait()

    def fetch(p):
        first, count = PARTS[p]
        at = pl.ds(first, count)
        slots = range(first, first + count)

        def held(k, j):
            entry = meta_s[place.yi(k), 0, j]
            return zbuf[entry // ROWS, lax.rem(entry, ROWS)]

        copies = []
        for n, k in enumerate(AROUND):
            for j in slots:
                ysend[n, j] = held(k, j)
            copies.append(net.send(ysend.at[n, at], yrecv.at[n, at], place.at_y(k)))
        yield
        for copy in copies:
            copy.wait_recv()
        for j in slots:
            column = meta_s[y, 1, j]
            value = lax.select(column == place.yi(-1), yrecv[0, j], yrecv[1, j])
            value = lax.select(column == place.yi(2), yrecv[2, j], value)
            rows[mp, j] = lax.select(column == y, held(0, j), value)

        def block(k):
            return rows.at[place.xi(k) * 2 + place.core, at]

        across = [net.send(block(0), block(0), place.sibling())]
        copies = [net.send(block(0), block(0), place.at_x(k)) for k in AROUND]
        yield
        for copy, k in zip(copies, (-1, 1, 2)):
            copy.wait_recv()
            across.append(net.send(block(k), block(k), place.sibling()))
        yield
        for copy in across:
            copy.wait_recv()

    def attend(p, i):
        scale = 1.0 / HD**0.5
        first, count = PARTS[p]
        part_rows = jnp.concatenate([rows[:, j].reshape(NLEN, E) for j in range(first, first + count)], axis=0)
        if i == Y_FIRST:
            rows_t[:, pl.ds(first * NLEN, count * NLEN)] = part_rows.T
        both = mm(part_rows, weights[i], ((1,), (0,))).astype(BF16)
        for c in range(count // 2):
            span_both = both[2 * c * NLEN:2 * (c + 1) * NLEN]
            span = pl.ds((first // 2 + c) * SPAN_LEN, SPAN_LEN)
            span_rows = pl.ds((first + 2 * c) * NLEN, 2 * NLEN)
            for h in range(2):
                cols = pl.ds((2 * i + h) * HD, HD)
                qh, gh = q[span, cols], g[span, cols]
                kh = span_both[:, h * HD:(h + 1) * HD]
                vh = span_both[:, half + h * HD:half + (h + 1) * HD]
                scores = mm(qh, kh, ((1,), (1,))) * scale
                top = jnp.max(scores, axis=-1, keepdims=True)
                grown = jnp.exp(scores - top)
                probs = grown / jnp.sum(grown, axis=-1, keepdims=True)
                low = probs.astype(BF16)
                att[span, cols] = mm(low, vh, ((1,), (0,))).astype(BF16)
                pgrad = mm(gh, vh, ((1,), (1,)))
                dot = jnp.sum(probs * pgrad, axis=-1, keepdims=True)
                sgrad = (scale * probs * (pgrad - dot)).astype(BF16)
                qg[span, cols] = mm(sgrad, kh, ((1,), (0,))).astype(BF16)
                grads[i, span_rows, pl.ds(h * HD, HD)] = mm(sgrad, qh, ((0,), (0,))).astype(BF16)
                grads[i, span_rows, pl.ds(half + h * HD, HD)] = mm(low, gh, ((0,), (0,))).astype(BF16)

    def slab_term(p):
        first, count = PARTS[p]
        total = None
        for i in range(2):
            term = mm(grads[i, pl.ds(first * NLEN, count * NLEN)], weights[i], ((1,), (1,)))
            total = term if total is None else total + term
        total = total.astype(BF16)
        for j in range(count):
            terms[:, first + j] = total[j * NLEN:(j + 1) * NLEN].reshape(GROUPS, TOK, E)

    def weight_term(i):
        total = mm(rows_t[...], grads[i], ((1,), (0,))).astype(BF16)
        for z in range(NZ):
            for u in range(UNITS):
                wgrad[i, z, u] = total[z * WROWS:(z + 1) * WROWS, u * HD:(u + 1) * HD]

    def give_back(p):
        at = pl.ds(*PARTS[p])
        order = AROUND + (0,)
        copies = [
            net.send(terms.at[place.xi(k) * 2 + (1 - place.core), at], theirs.at[n, at], place.sibling())
            for n, k in enumerate(order)
        ]
        yield
        crossing = []
        for n, k in enumerate(order):
            copies[n].wait_recv()
            block = terms.at[place.xi(k) * 2 + place.core, at]
            add_into(block, theirs.at[n, at])
            if k != 0:
                crossing.append(net.send(block, xrecv.at[n, at], place.at_x(k)))
        yield
        for copy in crossing:
            copy.wait_recv()
        total = terms[mp, at].astype(F32)
        for n in range(3):
            total = total + xrecv[n, at].astype(F32)
        ybuf[y, at] = total.astype(BF16)
        copies = [net.send(ybuf.at[y, at], ybuf.at[y, at], place.at_y(k)) for k in AROUND]
        yield
        for copy in copies:
            copy.wait_recv()

    def nothing(k):
        pass

    def sum_slabs():
        def prepare(k):
            shard = place.zi(k) * NY + y
            named = [
                (d, meta_s[d, 2, shard * 2 + r], meta_s[d, 3, shard * 2 + r]) for d in range(NY) for r in range(2)
            ]
            for row in range(ROWS):
                total = None
                for d, slot, slot_row in named:
                    weight = jnp.where(slot_row == row, 1.0, 0.0).astype(F32)
                    term = ybuf[d, slot].astype(F32) * weight
                    total = term if total is None else total + term
                share[(k + NZ) % NZ, row] = total.astype(BF16)

        yield from ring_scatter(
            net, NZ, place.at_z(1), place.at_z(-1), lambda k: share.at[(k + NZ) % NZ], prepare,
            lambda s: zl.at[s], lambda s: zr.at[s], ROW_HALVES,
        )
        state_out[...] = share[0].astype(F32)

    def result(res, i):
        return [
            net.local(res.at[:, u], out.at[:, :, pl.ds((2 * i + u % 2) * HD, HD)])
            for u, out in enumerate((kout, kout, vout, vout))
        ]

    def sum_z_first():
        total = wgrad.at[0]
        yield from ring_scatter(
            net, NZ, place.at_z(1), place.at_z(-1), lambda k: total.at[place.zi(k)], nothing,
            lambda s: wfl.at[s], lambda s: wfr.at[s], UNIT_HALVES,
        )
        wy[y] = total[place.z]
        copies = [net.send(wy.at[y], wy.at[y], place.at_y(k)) for k in AROUND]
        yield
        for copy in copies:
            copy.wait_recv()
        whole = wy[0].astype(F32)
        for d in range(1, NY):
            whole = whole + wy[d].astype(F32)
        wres[place.z] = whole.astype(BF16)
        yield from ring_gather(
            net, NZ, place.at_z(1), place.at_z(-1), lambda k: wres.at[place.zi(k)], UNIT_HALVES
        )
        done = result(wres, 0)
        yield
        for copy in done:
            copy.wait()

    def sum_y_first():
        total = wgrad.at[1]
        yield from ring_scatter(
            net, NY, place.at_y(1), place.at_y(-1), lambda k: total.at[:, place.yi(k)], nothing,
            lambda s: vyl.at[s], lambda s: vyr.at[s], ZBLOCK_HALVES,
        )
        yield from ring_scatter(
            net, NZ, place.at_z(1), place.at_z(-1), lambda k: total.at[place.zi(k), y], nothing,
            lambda s: vzl.at[s], lambda s: vzr.at[s], WROW_HALVES,
        )
        vres[place.z, y] = total[place.z, y]
        yield from ring_gather(
            net, NZ, place.at_z(1), place.at_z(-1), lambda k: vres.at[place.zi(k), y], WROW_HALVES
        )
        yield from ring_gather(
            net, NY, place.at_y(1), place.at_y(-1), lambda k: vres.at[:, place.yi(k)], ZBLOCK_HALVES
        )
        done = result(vres, 1)
        yield
        for copy in done:
            copy.wait()

    chains = {"A": sum_z_first(), "B": sum_y_first(), "Z": sum_slabs()}

    def load():
        for copy in loads:
            copy.wait()

    work = {"load": load, "w0": lambda: weight_term(Y_FIRST), "w1": lambda: weight_term(1 - Y_FIRST)}
    for p in range(len(PARTS)):
        chains[f"f{p}"] = fetch(p)
        chains[f"s{p}"] = give_back(p)
        work[f"t{p}"] = functools.partial(slab_term, p)
        work[f"a{p}0"] = functools.partial(attend, p, Y_FIRST)
        work[f"a{p}1"] = functools.partial(attend, p, 1 - Y_FIRST)
    for name in PLAN:
        if name in work:
            work[name]()
        else:
            next(chains[name], None)
    for chain in chains.values():
        for _ in chain:
            pass
    net.finish()


def fused(meta, states, queries, out_grad, key_weight, value_weight):
    slab = (TOK, E)
    block = (WROWS, HD)
    scratch = [
        pltpu.VMEM((NY, 8, 128), jnp.int32),
        pltpu.SMEM((NY, 8, 128), jnp.int32),
        pltpu.VMEM(queries.shape, BF16),
        pltpu.VMEM(out_grad.shape, BF16),
        pltpu.VMEM((2, E, LOCAL), BF16),
        pltpu.VMEM((NZ, ROWS) + slab, BF16),
        pltpu.VMEM((len(AROUND), SLOTS) + slab, BF16),
        pltpu.VMEM((len(AROUND), SLOTS) + slab, BF16),
        pltpu.VMEM((GROUPS, SLOTS) + slab, BF16),
        pltpu.VMEM((E, SLOTS * NLEN), BF16),
        pltpu.VMEM((2, SLOTS * NLEN, LOCAL), BF16),
        pltpu.VMEM((GROUPS, SLOTS) + slab, BF16),
        pltpu.VMEM((NX, SLOTS) + slab, BF16),
        pltpu.VMEM((len(AROUND), SLOTS) + slab, BF16),
        pltpu.VMEM((NY, SLOTS) + slab, BF16),
        pltpu.VMEM((NZ, ROWS) + slab, BF16),
        pltpu.VMEM((NZ // 2, ROWS) + slab, BF16),
        pltpu.VMEM((NZ // 2, ROWS) + slab, BF16),
        pltpu.VMEM((2, NZ, UNITS) + block, BF16),
        pltpu.VMEM((NZ // 2, UNITS) + block, BF16),
        pltpu.VMEM((NZ // 2, UNITS) + block, BF16),
        pltpu.VMEM((NY, UNITS) + block, BF16),
        pltpu.VMEM((NZ, UNITS) + block, BF16),
        pltpu.VMEM((NY // 2, NZ) + block, BF16),
        pltpu.VMEM((NY // 2, NZ) + block, BF16),
        pltpu.VMEM((NZ // 2,) + block, BF16),
        pltpu.VMEM((NZ // 2,) + block, BF16),
        pltpu.VMEM((NZ, UNITS) + block, BF16),
        pltpu.SemaphoreType.DMA((COPIES,)),
        pltpu.SemaphoreType.DMA((COPIES,)),
        pltpu.SemaphoreType.DMA((LOCALS,)),
    ]
    anywhere = pl.BlockSpec(memory_space=pl.ANY)
    vmem = pl.BlockSpec(memory_space=pltpu.VMEM)
    wshape = jax.ShapeDtypeStruct((NZ, WROWS, LOCAL), BF16)
    return pl.pallas_call(
        kernel,
        out_shape=[
            jax.ShapeDtypeStruct(queries.shape, BF16),
            jax.ShapeDtypeStruct(queries.shape, BF16),
            jax.ShapeDtypeStruct(states.shape, F32),
            wshape,
            wshape,
        ],
        in_specs=[vmem] + [anywhere] * 5,
        out_specs=[vmem] * 3 + [anywhere] * 2,
        scratch_shapes=scratch,
        compiler_params=pltpu.CompilerParams(
            collective_id=0, has_side_effects=True, vmem_limit_bytes=VMEM_LIMIT
        ),
        name="retrieve",
    )(meta, states, queries, out_grad, key_weight, value_weight)


def describe(nbr_shard, nbr_row):
    spans, count = nbr_shard.shape
    slots = jnp.arange(SLOTS, dtype=jnp.int32)
    spot = jnp.arange(count, dtype=jnp.int32)[:, None] + count * jnp.arange(spans, dtype=jnp.int32)[None, :]
    pick = (spot[:, :, None] == slots[None, None, :]).astype(jnp.int32)
    owners = jnp.sum(nbr_shard.T[:, :, None] * pick, axis=(0, 1))
    rows = jnp.sum(nbr_row.T[:, :, None] * pick, axis=(0, 1))
    entry = (owners // NY) * ROWS + rows
    column = lax.rem(owners, NY)
    same = jnp.logical_and(owners[:, None] == owners[None, :], slots[:, None] > slots[None, :])
    key = owners * 2 + jnp.sum(same.astype(jnp.int32), axis=1)
    hit = key[:, None] == jnp.arange(128, dtype=jnp.int32)[None, :]
    slot_of = jnp.sum(jnp.where(hit, slots[:, None], 0), axis=0)
    row_of = jnp.sum(jnp.where(hit, rows[:, None] + 1, 0), axis=0) - 1
    pad = (0, 128 - SLOTS)
    blank = jnp.zeros((128,), jnp.int32)
    return jnp.stack([jnp.pad(entry, pad), jnp.pad(column, pad), slot_of, row_of] + [blank] * 4)


def finish_kernel(*refs):
    count = len(refs) // 2
    for source, target in zip(refs[:count], refs[count:]):
        target[...] = source[...].astype(target.dtype)


def finish(arrays, types, steps):
    specs = []
    for array in arrays:
        rest = array.shape[1:]
        specs.append(
            pl.BlockSpec((array.shape[0] // steps,) + rest, lambda i, n=len(rest): (i,) + (0,) * n)
        )
    return pl.pallas_call(
        finish_kernel,
        grid=(steps,),
        out_shape=[jax.ShapeDtypeStruct(array.shape, kind) for array, kind in zip(arrays, types)],
        in_specs=specs,
        out_specs=specs,
        compiler_params=pltpu.CompilerParams(vmem_limit_bytes=VMEM_LIMIT),
        name="finish",
    )(*arrays)


def body(queries, states, key_weight, value_weight, nbr_shard, nbr_row, out_grad):
    arrays = fused(describe(nbr_shard, nbr_row), states, queries, out_grad, key_weight, value_weight)
    attended, query_grad, state_total, ktotal, vtotal = finish(arrays, (BF16, BF16, F32, F32, F32), FINISH_STEPS)
    return attended, query_grad, state_total, ktotal.reshape(E, LOCAL), vtotal.reshape(E, LOCAL)


def solution(mesh):
    placed = (
        P("dp", "mp"),
        P("dp", "mp", None),
        P(None, "mp"),
        P(None, "mp"),
        P("dp", None),
        P("dp", None),
        P("dp", "mp"),
    )
    return jax.shard_map(
        body,
        mesh=mesh,
        in_specs=placed,
        out_specs=(P("dp", "mp"), P("dp", "mp"), P("dp", "mp", None), P(None, "mp"), P(None, "mp")),
        check_vma=False,
    )
```

```python
import functools

import jax
import jax.numpy as jnp
from jax import lax
from jax.experimental import pallas as pl
from jax.experimental.pallas import tpu as pltpu
from jax.sharding import PartitionSpec as P

D = 4096
H = 32
HD = 128
NZ, NY, NX = 8, 4, 4
GROUPS = 8
SLOTS = 12
HALF = SLOTS // 2
ROWS = 8
TOK = 16
E = 896
VMEM_LIMIT = 56 * 1024 * 1024
FINISH_STEPS = 2
BF16 = jnp.bfloat16
F32 = jnp.float32


class Place:
    def __init__(self):
        dp, mp = lax.axis_index("dp"), lax.axis_index("mp")
        self.dp, self.mp = dp, mp
        self.z, self.y = dp // NY, lax.rem(dp, NY)
        self.x, self.core = mp // 2, lax.rem(mp, 2)

    def zi(self, k):
        return lax.rem(self.z + (k + NZ), NZ)

    def yi(self, k):
        return lax.rem(self.y + (k + NY), NY)

    def xi(self, k):
        return lax.rem(self.x + (k + NX), NX)

    def at_z(self, k):
        return (self.zi(k) * NY + self.y, self.mp)

    def at_y(self, k):
        return (self.z * NY + self.yi(k), self.mp)

    def at_x(self, k):
        return (self.dp, self.xi(k) * 2 + self.core)

    def sibling(self):
        return (self.dp, self.x * 2 + (1 - self.core))

    def partners(self):
        return [
            self.at_z(1), self.at_z(-1), self.at_y(1), self.at_y(-1), self.at_y(2),
            self.at_x(1), self.at_x(-1), self.at_x(2), self.sibling(),
        ]


class Net:
    def __init__(self, send_sems, recv_sems, local_sems):
        self.send_sems, self.recv_sems, self.local_sems = send_sems, recv_sems, local_sems
        self.sent = []
        self.locals = 0

    def send(self, src, dst, device):
        number = len(self.sent)
        copy = pltpu.make_async_remote_copy(
            src_ref=src,
            dst_ref=dst,
            send_sem=self.send_sems.at[number],
            recv_sem=self.recv_sems.at[number],
            device_id=device,
            device_id_type=pl.DeviceIdType.MESH,
        )
        copy.start()
        self.sent.append(copy)
        return copy

    def local(self, src, dst):
        copy = pltpu.make_async_copy(src, dst, self.local_sems.at[self.locals])
        copy.start()
        self.locals += 1
        return copy

    def finish(self):
        for copy in self.sent:
            copy.wait_send()


def greet(place):
    barrier = pltpu.get_barrier_semaphore()
    partners = place.partners()
    for device in partners:
        pl.semaphore_signal(barrier, inc=1, device_id=device, device_id_type=pl.DeviceIdType.MESH)
    pl.semaphore_wait(barrier, len(partners))


def part(ref, bounds):
    first, count = bounds
    return ref.at[pl.ds(first, count)]


def ring_gather(net, n, right, left, slot, halves, landed=None):
    half_r, half_l = halves
    whole = (half_r[0], half_r[1] + half_l[1])
    far = n // 2
    for step in range(1, far + 1):
        piece_r = half_r if step == far else whole
        piece_l = half_l if step == far else whole
        block_r, block_l = part(slot(1 - step), piece_r), part(slot(step - 1), piece_l)
        to_right = net.send(block_r, block_r, right)
        to_left = net.send(block_l, block_l, left)
        yield
        to_right.wait_recv()
        if landed is not None:
            landed(part(slot(-step), piece_r))
        to_left.wait_recv()
        if landed is not None:
            landed(part(slot(step), piece_l))


def add_into(target, *others):
    total = target[...].astype(F32)
    for other in others:
        total = total + other[...].astype(F32)
    target[...] = total.astype(target.dtype)


def ring_scatter(net, n, right, left, total, prepare, from_left, from_right, halves):
    half_r, half_l = halves
    whole = (half_r[0], half_r[1] + half_l[1])
    far = n // 2
    prepare(far)
    to_right = [net.send(part(total(far), half_r), part(from_left(0), half_r), right)]
    to_left = [net.send(part(total(far), half_l), part(from_right(0), half_l), left)]
    for step in range(1, far):
        k = far - step
        prepare(k)
        prepare(-k)
        early_r, early_l = [], []
        if step == 1:
            early_r.append(net.send(part(total(k), half_l), part(from_left(step), half_l), right))
            early_l.append(net.send(part(total(-k), half_r), part(from_right(step), half_r), left))
        piece_r = half_r if step == 1 else whole
        piece_l = half_l if step == 1 else whole
        yield
        for copy in to_right:
            copy.wait_recv()
        add_into(part(total(k), piece_r), part(from_left(step - 1), piece_r))
        to_right = early_r + [net.send(part(total(k), piece_r), part(from_left(step), piece_r), right)]
        for copy in to_left:
            copy.wait_recv()
        add_into(part(total(-k), piece_l), part(from_right(step - 1), piece_l))
        to_left = early_l + [net.send(part(total(-k), piece_l), part(from_right(step), piece_l), left)]
    prepare(0)
    yield
    for copy in to_right + to_left:
        copy.wait_recv()
    add_into(total(0), from_left(far - 1), from_right(far - 1))


ROW_HALVES = ((0, ROWS // 2), (ROWS // 2, ROWS // 2))
SPAN_LEN = 64
LOCAL = 512
NLEN = GROUPS * TOK
PARTS = ((0, 4), (4, 4), (8, 2), (10, 2))
WROWS = E // NZ
UNITS = 4
Y_FIRST = 1
UNIT_HALVES = ((0, UNITS // 2), (UNITS // 2, UNITS // 2))
ZBLOCK_HALVES = ((0, NZ // 2), (NZ // 2, NZ // 2))
WROW_HALVES = ((0, 64), (64, WROWS - 64))
COPIES = 160
LOCALS = 32
AROUND = (1, -1, 2)
PLAN = (
    "f2", "f3", "load", "f1", "f2", "f3", "f0", "f2", "f1", "f2", "a20", "f3", "a21", "t2", "f3", "s2", "f0",
    "a30", "s2", "f1", "a31", "f1", "a10", "f0", "a11", "t1", "f0", "a00", "s1", "w0", "B", "s1", "a01", "w1",
    "A", "t3", "s3", "B", "t0", "s0", "s3", "s1", "s2", "A", "s0", "B", "A", "s3", "B", "s0", "s1", "B", "A",
    "B", "s2", "A", "s3", "B", "s0", "Z", "B", "A", "B", "Z", "B", "A", "Z", "B", "A", "Z", "B", "A", "B",
    "B", "Z", "A", "A",
)


def mm(a, b, dims):
    return lax.dot_general(a, b, (dims, ((), ())), preferred_element_type=F32)


def kernel(
    meta_in, states, queries, out_grad, key_weight, value_weight,
    att, qg, state_out, kout, vout,
    meta_v, meta_s, q, g, weights, zbuf, ysend, yrecv, rows, rows_t, grads, terms, theirs, xrecv,
    ybuf, share, zl, zr, wgrad, wfl, wfr, wy, wres, vyl, vyr, vzl, vzr, vres,
    send_sems, recv_sems, local_sems,
):
    place = Place()
    net = Net(send_sems, recv_sems, local_sems)
    y, mp = place.y, place.mp
    load_states = net.local(states, zbuf.at[place.z])
    own_meta = net.local(meta_in, meta_v.at[y])
    loads = []
    half = LOCAL // 2
    for i in range(2):
        from_cols = pl.ds(i * half, half)
        loads.append(net.local(key_weight.at[:, from_cols], weights.at[i, :, pl.ds(0, half)]))
        loads.append(net.local(value_weight.at[:, from_cols], weights.at[i, :, pl.ds(half, half)]))
    loads.append(net.local(queries, q))
    loads.append(net.local(out_grad, g))
    greet(place)

    meta_copies = [net.send(meta_in, meta_v.at[y], place.at_y(k)) for k in AROUND]
    load_states.wait()
    for turn, _ in enumerate(
        ring_gather(net, NZ, place.at_z(1), place.at_z(-1), lambda k: zbuf.at[place.zi(k)], ROW_HALVES)
    ):
        if turn == 1:
            own_meta.wait()
            for copy in meta_copies:
                copy.wait_recv()
            to_smem = net.local(meta_v, meta_s)
    to_smem.wait()

    def fetch(p):
        first, count = PARTS[p]
        at = pl.ds(first, count)
        slots = range(first, first + count)

        def held(k, j):
            entry = meta_s[place.yi(k), 0, j]
            return zbuf[entry // ROWS, lax.rem(entry, ROWS)]

        copies = []
        for n, k in enumerate(AROUND):
            for j in slots:
                ysend[n, j] = held(k, j)
            copies.append(net.send(ysend.at[n, at], yrecv.at[n, at], place.at_y(k)))
        yield
        for copy in copies:
            copy.wait_recv()
        for j in slots:
            column = meta_s[y, 1, j]
            value = lax.select(column == place.yi(-1), yrecv[0, j], yrecv[1, j])
            value = lax.select(column == place.yi(2), yrecv[2, j], value)
            rows[mp, j] = lax.select(column == y, held(0, j), value)

        def block(k):
            return rows.at[place.xi(k) * 2 + place.core, at]

        across = [net.send(block(0), block(0), place.sibling())]
        copies = [net.send(block(0), block(0), place.at_x(k)) for k in AROUND]
        yield
        for copy, k in zip(copies, (-1, 1, 2)):
            copy.wait_recv()
            across.append(net.send(block(k), block(k), place.sibling()))
        yield
        for copy in across:
            copy.wait_recv()

    def attend(p, i):
        scale = 1.0 / HD**0.5
        first, count = PARTS[p]
        part_rows = jnp.concatenate([rows[:, j].reshape(NLEN, E) for j in range(first, first + count)], axis=0)
        if i == Y_FIRST:
            rows_t[:, pl.ds(first * NLEN, count * NLEN)] = part_rows.T
        both = mm(part_rows, weights[i], ((1,), (0,))).astype(BF16)
        for c in range(count // 2):
            span_both = both[2 * c * NLEN:2 * (c + 1) * NLEN]
            span = pl.ds((first // 2 + c) * SPAN_LEN, SPAN_LEN)
            span_rows = pl.ds((first + 2 * c) * NLEN, 2 * NLEN)
            for h in range(2):
                cols = pl.ds((2 * i + h) * HD, HD)
                qh, gh = q[span, cols], g[span, cols]
                kh = span_both[:, h * HD:(h + 1) * HD]
                vh = span_both[:, half + h * HD:half + (h + 1) * HD]
                scores = mm(qh, kh, ((1,), (1,))) * scale
                top = jnp.max(scores, axis=-1, keepdims=True)
                grown = jnp.exp(scores - top)
                probs = grown * (1.0 / jnp.sum(grown, axis=-1, keepdims=True))
                low = probs.astype(BF16)
                att[span, cols] = mm(low, vh, ((1,), (0,))).astype(BF16)
                pgrad = mm(gh, vh, ((1,), (1,)))
                dot = jnp.sum(probs * pgrad, axis=-1, keepdims=True)
                sgrad = (scale * probs * (pgrad - dot)).astype(BF16)
                qg[span, cols] = mm(sgrad, kh, ((1,), (0,))).astype(BF16)
                grads[i, span_rows, pl.ds(h * HD, HD)] = mm(sgrad, qh, ((0,), (0,))).astype(BF16)
                grads[i, span_rows, pl.ds(half + h * HD, HD)] = mm(low, gh, ((0,), (0,))).astype(BF16)

    def slab_term(p):
        first, count = PARTS[p]
        total = None
        for i in range(2):
            term = mm(grads[i, pl.ds(first * NLEN, count * NLEN)], weights[i], ((1,), (1,)))
            total = term if total is None else total + term
        total = total.astype(BF16)
        for j in range(count):
            terms[:, first + j] = total[j * NLEN:(j + 1) * NLEN].reshape(GROUPS, TOK, E)

    def weight_term(i):
        total = mm(rows_t[...], grads[i], ((1,), (0,))).astype(BF16)
        for z in range(NZ):
            for u in range(UNITS):
                wgrad[i, z, u] = total[z * WROWS:(z + 1) * WROWS, u * HD:(u + 1) * HD]

    def give_back(p):
        at = pl.ds(*PARTS[p])
        order = AROUND + (0,)
        copies = [
            net.send(terms.at[place.xi(k) * 2 + (1 - place.core), at], theirs.at[n, at], place.sibling())
            for n, k in enumerate(order)
        ]
        yield
        crossing = []
        for n, k in enumerate(order):
            copies[n].wait_recv()
            block = terms.at[place.xi(k) * 2 + place.core, at]
            add_into(block, theirs.at[n, at])
            if k != 0:
                crossing.append(net.send(block, xrecv.at[n, at], place.at_x(k)))
        yield
        for copy in crossing:
            copy.wait_recv()
        total = terms[mp, at].astype(F32)
        for n in range(3):
            total = total + xrecv[n, at].astype(F32)
        ybuf[y, at] = total.astype(BF16)
        copies = [net.send(ybuf.at[y, at], ybuf.at[y, at], place.at_y(k)) for k in AROUND]
        yield
        for copy in copies:
            copy.wait_recv()

    def nothing(k):
        pass

    def sum_slabs():
        def prepare(k):
            shard = place.zi(k) * NY + y
            named = [
                (d, meta_s[d, 2, shard * 2 + r], meta_s[d, 3, shard * 2 + r]) for d in range(NY) for r in range(2)
            ]
            for row in range(ROWS):
                total = None
                for d, slot, slot_row in named:
                    weight = jnp.where(slot_row == row, 1.0, 0.0).astype(F32)
                    term = ybuf[d, slot].astype(F32) * weight
                    total = term if total is None else total + term
                share[(k + NZ) % NZ, row] = total.astype(BF16)

        yield from ring_scatter(
            net, NZ, place.at_z(1), place.at_z(-1), lambda k: share.at[(k + NZ) % NZ], prepare,
            lambda s: zl.at[s], lambda s: zr.at[s], ROW_HALVES,
        )
        state_out[...] = share[0].astype(F32)

    def result(res, i):
        return [
            net.local(res.at[:, u], out.at[:, :, pl.ds((2 * i + u % 2) * HD, HD)])
            for u, out in enumerate((kout, kout, vout, vout))
        ]

    def sum_z_first():
        total = wgrad.at[0]
        yield from ring_scatter(
            net, NZ, place.at_z(1), place.at_z(-1), lambda k: total.at[place.zi(k)], nothing,
            lambda s: wfl.at[s], lambda s: wfr.at[s], UNIT_HALVES,
        )
        wy[y] = total[place.z]
        copies = [net.send(wy.at[y], wy.at[y], place.at_y(k)) for k in AROUND]
        yield
        for copy in copies:
            copy.wait_recv()
        whole = wy[0].astype(F32)
        for d in range(1, NY):
            whole = whole + wy[d].astype(F32)
        wres[place.z] = whole.astype(BF16)
        yield from ring_gather(
            net, NZ, place.at_z(1), place.at_z(-1), lambda k: wres.at[place.zi(k)], UNIT_HALVES
        )
        done = result(wres, 0)
        yield
        for copy in done:
            copy.wait()

    def sum_y_first():
        total = wgrad.at[1]
        yield from ring_scatter(
            net, NY, place.at_y(1), place.at_y(-1), lambda k: total.at[:, place.yi(k)], nothing,
            lambda s: vyl.at[s], lambda s: vyr.at[s], ZBLOCK_HALVES,
        )
        yield from ring_scatter(
            net, NZ, place.at_z(1), place.at_z(-1), lambda k: total.at[place.zi(k), y], nothing,
            lambda s: vzl.at[s], lambda s: vzr.at[s], WROW_HALVES,
        )
        vres[place.z, y] = total[place.z, y]
        yield from ring_gather(
            net, NZ, place.at_z(1), place.at_z(-1), lambda k: vres.at[place.zi(k), y], WROW_HALVES
        )
        yield from ring_gather(
            net, NY, place.at_y(1), place.at_y(-1), lambda k: vres.at[:, place.yi(k)], ZBLOCK_HALVES
        )
        done = result(vres, 1)
        yield
        for copy in done:
            copy.wait()

    chains = {"A": sum_z_first(), "B": sum_y_first(), "Z": sum_slabs()}

    def load():
        for copy in loads:
            copy.wait()

    work = {"load": load, "w0": lambda: weight_term(Y_FIRST), "w1": lambda: weight_term(1 - Y_FIRST)}
    for p in range(len(PARTS)):
        chains[f"f{p}"] = fetch(p)
        chains[f"s{p}"] = give_back(p)
        work[f"t{p}"] = functools.partial(slab_term, p)
        work[f"a{p}0"] = functools.partial(attend, p, Y_FIRST)
        work[f"a{p}1"] = functools.partial(attend, p, 1 - Y_FIRST)
    for name in PLAN:
        if name in work:
            work[name]()
        else:
            next(chains[name], None)
    for chain in chains.values():
        for _ in chain:
            pass
    net.finish()


def fused(meta, states, queries, out_grad, key_weight, value_weight):
    slab = (TOK, E)
    block = (WROWS, HD)
    scratch = [
        pltpu.VMEM((NY, 8, 128), jnp.int32),
        pltpu.SMEM((NY, 8, 128), jnp.int32),
        pltpu.VMEM(queries.shape, BF16),
        pltpu.VMEM(out_grad.shape, BF16),
        pltpu.VMEM((2, E, LOCAL), BF16),
        pltpu.VMEM((NZ, ROWS) + slab, BF16),
        pltpu.VMEM((len(AROUND), SLOTS) + slab, BF16),
        pltpu.VMEM((len(AROUND), SLOTS) + slab, BF16),
        pltpu.VMEM((GROUPS, SLOTS) + slab, BF16),
        pltpu.VMEM((E, SLOTS * NLEN), BF16),
        pltpu.VMEM((2, SLOTS * NLEN, LOCAL), BF16),
        pltpu.VMEM((GROUPS, SLOTS) + slab, BF16),
        pltpu.VMEM((NX, SLOTS) + slab, BF16),
        pltpu.VMEM((len(AROUND), SLOTS) + slab, BF16),
        pltpu.VMEM((NY, SLOTS) + slab, BF16),
        pltpu.VMEM((NZ, ROWS) + slab, BF16),
        pltpu.VMEM((NZ // 2, ROWS) + slab, BF16),
        pltpu.VMEM((NZ // 2, ROWS) + slab, BF16),
        pltpu.VMEM((2, NZ, UNITS) + block, BF16),
        pltpu.VMEM((NZ // 2, UNITS) + block, BF16),
        pltpu.VMEM((NZ // 2, UNITS) + block, BF16),
        pltpu.VMEM((NY, UNITS) + block, BF16),
        pltpu.VMEM((NZ, UNITS) + block, BF16),
        pltpu.VMEM((NY // 2, NZ) + block, BF16),
        pltpu.VMEM((NY // 2, NZ) + block, BF16),
        pltpu.VMEM((NZ // 2,) + block, BF16),
        pltpu.VMEM((NZ // 2,) + block, BF16),
        pltpu.VMEM((NZ, UNITS) + block, BF16),
        pltpu.SemaphoreType.DMA((COPIES,)),
        pltpu.SemaphoreType.DMA((COPIES,)),
        pltpu.SemaphoreType.DMA((LOCALS,)),
    ]
    anywhere = pl.BlockSpec(memory_space=pl.ANY)
    vmem = pl.BlockSpec(memory_space=pltpu.VMEM)
    wshape = jax.ShapeDtypeStruct((NZ, WROWS, LOCAL), BF16)
    return pl.pallas_call(
        kernel,
        out_shape=[
            jax.ShapeDtypeStruct(queries.shape, BF16),
            jax.ShapeDtypeStruct(queries.shape, BF16),
            jax.ShapeDtypeStruct(states.shape, F32),
            wshape,
            wshape,
        ],
        in_specs=[vmem] + [anywhere] * 5,
        out_specs=[vmem] * 3 + [anywhere] * 2,
        scratch_shapes=scratch,
        compiler_params=pltpu.CompilerParams(
            collective_id=0, has_side_effects=True, vmem_limit_bytes=VMEM_LIMIT
        ),
        name="retrieve",
    )(meta, states, queries, out_grad, key_weight, value_weight)


def describe(nbr_shard, nbr_row):
    spans, count = nbr_shard.shape
    slots = jnp.arange(SLOTS, dtype=jnp.int32)
    spot = jnp.arange(count, dtype=jnp.int32)[:, None] + count * jnp.arange(spans, dtype=jnp.int32)[None, :]
    pick = (spot[:, :, None] == slots[None, None, :]).astype(jnp.int32)
    owners = jnp.sum(nbr_shard.T[:, :, None] * pick, axis=(0, 1))
    rows = jnp.sum(nbr_row.T[:, :, None] * pick, axis=(0, 1))
    entry = (owners // NY) * ROWS + rows
    column = lax.rem(owners, NY)
    same = jnp.logical_and(owners[:, None] == owners[None, :], slots[:, None] > slots[None, :])
    key = owners * 2 + jnp.sum(same.astype(jnp.int32), axis=1)
    hit = key[:, None] == jnp.arange(128, dtype=jnp.int32)[None, :]
    slot_of = jnp.sum(jnp.where(hit, slots[:, None], 0), axis=0)
    row_of = jnp.sum(jnp.where(hit, rows[:, None] + 1, 0), axis=0) - 1
    pad = (0, 128 - SLOTS)
    blank = jnp.zeros((128,), jnp.int32)
    return jnp.stack([jnp.pad(entry, pad), jnp.pad(column, pad), slot_of, row_of] + [blank] * 4)


def finish_kernel(*refs):
    count = len(refs) // 2
    for source, target in zip(refs[:count], refs[count:]):
        target[...] = source[...].astype(target.dtype)


def finish(arrays, types, steps):
    specs = []
    for array in arrays:
        rest = array.shape[1:]
        specs.append(
            pl.BlockSpec((array.shape[0] // steps,) + rest, lambda i, n=len(rest): (i,) + (0,) * n)
        )
    return pl.pallas_call(
        finish_kernel,
        grid=(steps,),
        out_shape=[jax.ShapeDtypeStruct(array.shape, kind) for array, kind in zip(arrays, types)],
        in_specs=specs,
        out_specs=specs,
        compiler_params=pltpu.CompilerParams(vmem_limit_bytes=VMEM_LIMIT),
        name="finish",
    )(*arrays)


def body(queries, states, key_weight, value_weight, nbr_shard, nbr_row, out_grad):
    arrays = fused(describe(nbr_shard, nbr_row), states, queries, out_grad, key_weight, value_weight)
    attended, query_grad, state_total, ktotal, vtotal = finish(arrays, (BF16, BF16, F32, F32, F32), FINISH_STEPS)
    return attended, query_grad, state_total, ktotal.reshape(E, LOCAL), vtotal.reshape(E, LOCAL)


def solution(mesh):
    placed = (
        P("dp", "mp"),
        P("dp", "mp", None),
        P(None, "mp"),
        P(None, "mp"),
        P("dp", None),
        P("dp", None),
        P("dp", "mp"),
    )
    return jax.shard_map(
        body,
        mesh=mesh,
        in_specs=placed,
        out_specs=(P("dp", "mp"), P("dp", "mp"), P("dp", "mp", None), P(None, "mp"), P(None, "mp")),
        check_vma=False,
    )
```
